32 devices in a mesh: groups: 2 (over y), ep: 8 (over z, core), tp: 2 (over x).
Axes of the slice: x: 2, y: 2, z: 4, core: 2. Of those that a mesh axis runs over, the one named last changes fastest.
Arguments:
- queries: bfloat16 [1024, 4096], P(('groups', 'ep', 'tp')), parts along dimension 0, may hold values from -6 to 6
- new_kv: bfloat16 [1024, 4, 256], P(('groups', 'ep', 'tp')), parts along dimension 0, may hold values from -6 to 6
- cache: bfloat16 [1024, 4, 32, 256], P(('groups', 'ep', 'tp')), parts along dimension 0, may hold values from -6 to 6
- lengths: int32 [1024], P(('groups', 'ep', 'tp')), parts along dimension 0, may hold values from 2 to 32, as said below
- out_weight: bfloat16 [4096, 2048], P('tp'), may hold values from -0.09375 to 0.09375
- residual: bfloat16 [1024, 2048], P(('groups', 'ep'), 'tp'), parts along dimension 0, may hold values from -10 to 10
- norm_gain: float32 [2048], replicated, may hold values from 0.25 to 1.75
- expert_ids: int32 [1024, 8], P(('groups', 'ep')), parts along dimension 0, may hold values from 0 to 15, all different within a row; in each aligned block of 64 rows (0 to 63, 64 to 127, ...) at most 64 rows name the same one
- expert_gates: float32 [1024, 8], P(('groups', 'ep')), parts along dimension 0, may hold values from 0.05 to 1
- w_gate: bfloat16 [2048, 12288], P(None, ('ep', 'tp')), may hold values from -0.125 to 0.125
- w_up: bfloat16 [2048, 12288], P(None, ('ep', 'tp')), may hold values from -0.125 to 0.125
- w_down: bfloat16 [12288, 2048], P(('ep', 'tp')), may hold values from -0.21875 to 0.21875
Outputs:
- layer_out: bfloat16 [1024, 2048], P(('groups', 'ep'), 'tp'), parts along dimension 0
The draws below stay inside these ranges and needn't reach their ends.
There are 2 independent parts, one for each index of `groups`. The reference program is written for one: setup_inputs(seed, part) draws one part's arguments, and reference() takes and returns one part's arrays. A program takes and returns all parts, laid end to end along the dimension named above; an argument that names none is the same for every part. Nothing has to cross between parts.
Inputs may be any that keep to these rules, and one draw needn't show every extreme that they name: `expert_ids`: each row names 8 different experts; in the 64 rows of one index of ep (aligned blocks of rows) no expert is named by more than 64 rows, a bound that some block reaches. `lengths`: some row has the full 32 positions.
All inputs are finite; a program needn't handle non-finite values.
Results may differ from the reference program's by a relative error of at most 0.009.
Values may be sent and summed in bfloat16 or wider, within the bound.
A program may use at most 128 MiB of HBM per device.

```python
import math
import jax
import jax.numpy as jnp
import numpy as np
from jax import lax

D = 2048
HD = 128
HEADS = 32
KVH = 4
MOE_FF = 768
TOPK = 8
ROWS_DEV = 64
CTX = 32
ROWS = 512
EXPERTS = 16
CAP = 64
N_EP = 8


def draw_queries(key, part):
    key = jax.random.fold_in(key, 5)
    values = jnp.clip(jax.random.normal(key, (ROWS, HEADS * HD), jnp.float32), -6.0, 6.0)
    return values.astype(jnp.bfloat16)


def draw_cache(key, part):
    key = jax.random.fold_in(key, 7)
    array_shape = (ROWS, KVH, CTX, 2 * HD)
    values = jnp.clip(jax.random.normal(key, array_shape, jnp.float32), -6.0, 6.0)
    return values.astype(jnp.bfloat16)


def draw_lengths(key, part):
    key = jax.random.fold_in(key, 9)
    draw_key, pick_key = jax.random.split(key)
    counts = jax.random.randint(draw_key, (ROWS,), 2, CTX + 1)
    chosen_row = jax.random.randint(pick_key, (), 0, ROWS)
    return jnp.where(jnp.arange(ROWS) == chosen_row, CTX, counts).astype(jnp.int32)


def draw_residual(key, part):
    key = jax.random.fold_in(key, 13)
    row_key, noise_key = jax.random.split(key, 2)
    row_scale = jnp.exp(jax.random.uniform(row_key, (ROWS, 1), jnp.float32, -2.3026, -0.5108))
    column_pos = jnp.arange(D, dtype=jnp.float32)[None, :] / (D - 1)
    col_scale = 3.0 ** column_pos
    values = row_scale * col_scale * jnp.clip(jax.random.normal(noise_key, (ROWS, D), jnp.float32), -4.0, 4.0)
    return values.astype(jnp.bfloat16)


def levels(rng, shape, pieces, smallest, top_value):
    def one(axis_at, shards_of):
        steps = jax.random.uniform(jax.random.fold_in(jax.random.fold_in(rng, 6), axis_at), (shards_of,), jnp.float32, smallest / len(pieces), top_value / len(pieces))
        return jnp.repeat(jnp.exp(steps), shape[axis_at] // shards_of).reshape((-1,) + (1,) * (len(shape) - axis_at - 1))

    gain = one(*pieces[0])
    for cut in pieces[1:]:
        gain = gain * one(*cut)
    return gain


def shared_out(rng, own, number, rows, count, top, bound, skew):
    order = jax.random.permutation(rng, count)
    packed, usual = load_shares(count, rows * top, bound, skew, True), load_shares(count, rows * top, bound, skew, False)
    places = jnp.arange(count)

    def named(sizes, offset_by):
        used = int((sizes > 0).sum())
        fixed = max(1, used // 4)
        passed = fixed + (places - fixed + offset_by * (used - fixed)) % max(1, count - fixed)
        return jnp.zeros((count,), jnp.int32).at[order[jnp.where(places < fixed, places, passed)]].set(jnp.asarray(sizes, jnp.int32))

    sizes = jnp.where(number % 4 == 0, named(packed, number // 4), named(usual, number - number // 4 - 1))
    mixed = jax.random.permutation(jax.random.fold_in(own, 3), count)
    giver, sink = mixed[0:count // 2 * 2:2], mixed[1:count // 2 * 2:2]
    slack = jnp.minimum(sizes[giver] - 1, bound - sizes[sink]) // 2
    slack = jnp.where((giver == order[0]) | (sink == order[0]) | (sizes[sink] == 0), 0, jnp.maximum(slack, 0))
    passed = jax.random.randint(jax.random.fold_in(own, 4), (count // 2,), 0, 1 << 20) % (slack + 1)
    sizes = sizes.at[giver].add(-passed).at[sink].add(passed)
    labels = jnp.searchsorted(jnp.cumsum(sizes), jnp.arange(rows * top), side="right").astype(jnp.int32)
    table = labels.reshape(top, rows).T
    table = table[jax.random.permutation(jax.random.fold_in(own, 1), rows)]
    offset_by = jax.random.randint(jax.random.fold_in(own, 2), (rows, 1), 0, top)
    return jnp.take_along_axis(table, (jnp.arange(top)[None, :] + offset_by) % top, axis=1)


def load_shares(number_of, total, most, skew, full):
    loads = [(1 << 20) // math.isqrt(rank ** skew) + 1 for rank in range(1, number_of + 1)]
    largest = most if full else min(most, max(-(-total // number_of), total * loads[0] // sum(loads)))
    least = 1 if total - largest >= number_of - 1 else 0
    holding, rest = [largest] + [least] * (number_of - 1), total - largest - least * (number_of - 1)
    while rest > 0:
        candidates = [i for i in range(1, number_of) if holding[i] < largest] or [i for i in range(1, number_of) if holding[i] < most]
        whole, left = sum([loads[i] for i in candidates]), rest
        for i in candidates:
            addition = min(most - holding[i], max(1, left * loads[i] // whole), rest)
            holding[i] = holding[i] + addition
            rest = rest - addition
    return np.array(holding)


def bell_draw(own_key, dims, deviation, reach, pieces=(), kind=jnp.bfloat16):
    drawn = deviation * jax.random.normal(own_key, dims, jnp.float32)
    if pieces:
        drawn = drawn * levels(own_key, dims, pieces, -0.22, 0.18)
    return jnp.clip(drawn, -reach, reach).astype(kind)


def setup_inputs(seed: int = 0, part: int = 0) -> dict:
    key_list = jax.random.split(jax.random.key(seed), 13)
    part_keys = jax.random.split(jax.random.fold_in(key_list[12], part), 13)
    queries = draw_queries(jax.random.fold_in(jax.random.fold_in(key_list[12], part), 71), part)
    new_kv = bell_draw(part_keys[1], (ROWS, KVH, 2 * HD), 1.0, 6.0, ((0, 16),))
    cache = draw_cache(jax.random.fold_in(jax.random.fold_in(key_list[12], part), 71), part)
    lengths = draw_lengths(jax.random.fold_in(jax.random.fold_in(key_list[12], part), 71), part)
    out_weight = bell_draw(key_list[4], (HEADS * HD, D), (HEADS * HD) ** -0.5, 0.09375, ((0, 2),))
    residual = draw_residual(jax.random.fold_in(jax.random.fold_in(key_list[12], part), 71), part)
    norm_gain = jnp.clip(1.0 + 0.15 * jax.random.normal(key_list[6], (D,), jnp.float32), 0.25, 1.75)
    expert_ids_keys = jax.random.split(jax.random.fold_in(part_keys[7], 1), ROWS // ROWS_DEV)
    expert_ids_turns = jax.random.permutation(jax.random.fold_in(part_keys[7], 3), ROWS // ROWS_DEV)
    expert_ids = jax.vmap(lambda own, number: shared_out(jax.random.fold_in(part_keys[7], 2), own, number, ROWS_DEV, EXPERTS, TOPK, CAP, 2))(expert_ids_keys, expert_ids_turns).reshape((ROWS, TOPK))
    expert_gates = jnp.clip(jnp.exp(math.log(1.0) - 2.9957323 * jax.random.uniform(part_keys[8], (ROWS, TOPK), jnp.float32) ** levels(part_keys[8], (ROWS, TOPK), ((0, 8),), -0.2, 0.2)), 0.05, 1.0)
    w_gate = bell_draw(key_list[9], (D, EXPERTS * MOE_FF), D ** -0.5, 0.125, ((1, 16),))
    w_up = bell_draw(key_list[10], (D, EXPERTS * MOE_FF), D ** -0.5, 0.125, ((1, 16),))
    w_down = bell_draw(key_list[11], (EXPERTS * MOE_FF, D), MOE_FF ** -0.5, 0.21875, ((0, 16),))
    return dict(queries=queries, new_kv=new_kv, cache=cache, lengths=lengths, out_weight=out_weight, residual=residual, norm_gain=norm_gain, expert_ids=expert_ids, expert_gates=expert_gates, w_gate=w_gate, w_up=w_up, w_down=w_down)


epsilon = 1e-06

def attention_rows(queries, new_kv, cache, lengths):
    row_count = queries.shape[0]
    group_size = HEADS // KVH
    query = queries.astype(jnp.float32).reshape(row_count, KVH, group_size, HD)
    key_part = cache[..., :HD].astype(jnp.float32)
    value_part = cache[..., HD:].astype(jnp.float32)
    new_key = new_kv[..., :HD].astype(jnp.float32)
    new_value = new_kv[..., HD:].astype(jnp.float32)
    score_scale = 1.0 / math.sqrt(HD)
    scores = jnp.einsum('rgqd,rgcd->rgqc', query, key_part) * score_scale
    fresh_score = jnp.einsum('rgqd,rgd->rgq', query, new_key) * score_scale
    is_valid = (jnp.arange(CTX, dtype=jnp.int32)[None, :] < lengths[:, None])[:, None, None, :]
    masked = jnp.where(is_valid, scores, -1e+30)
    row_max = jnp.maximum(lax.optimization_barrier(jnp.max(masked, -1)), fresh_score)
    exp_terms = jnp.where(is_valid, jnp.exp(masked - row_max[..., None]), 0.0)
    fresh_exp = jnp.exp(fresh_score - row_max)
    totals = lax.optimization_barrier(jnp.sum(exp_terms, -1)) + fresh_exp
    weights = lax.optimization_barrier((exp_terms / totals[..., None]).astype(jnp.bfloat16)).astype(jnp.float32)
    fresh_weight = lax.optimization_barrier((fresh_exp / totals).astype(jnp.bfloat16)).astype(jnp.float32)
    mixed = jnp.einsum('rgqc,rgcd->rgqd', weights, value_part)
    mixed = mixed + fresh_weight[..., None] * new_value[:, :, None, :]
    return mixed.astype(jnp.bfloat16).reshape(row_count, HEADS * HD)

def reference(queries, new_kv, cache, lengths, out_weight, residual, norm_gain, expert_ids, expert_gates, w_gate, w_up, w_down):
    attn_heads = attention_rows(queries, new_kv, cache, lengths)
    attn_out = jnp.dot(attn_heads, out_weight, preferred_element_type=jnp.float32)
    hidden = (residual.astype(jnp.float32) + attn_out).astype(jnp.bfloat16)
    hidden_f = hidden.astype(jnp.float32)
    inv_scale = lax.rsqrt(lax.optimization_barrier(jnp.mean(hidden_f * hidden_f, 1, keepdims=True)) + epsilon)
    normed = (hidden_f * inv_scale * norm_gain).astype(jnp.bfloat16)
    route_weights = expert_gates / lax.optimization_barrier(jnp.sum(expert_gates, 1, keepdims=True))
    limit = N_EP * CAP

    def one_expert(carry, expert):
        matches = expert_ids == expert
        chosen = jnp.any(matches, 1)
        gate_of = lax.optimization_barrier(jnp.sum(jnp.where(matches, route_weights, 0.0), 1))
        picked = jnp.nonzero(chosen, size=limit, fill_value=0)[0]
        live = jnp.arange(limit) < jnp.sum(chosen.astype(jnp.int32))
        inputs = normed[picked]
        columns = (expert * MOE_FF).astype(jnp.int32)
        gate_cols = lax.dynamic_slice_in_dim(w_gate, columns, MOE_FF, 1)
        up_cols = lax.dynamic_slice_in_dim(w_up, columns, MOE_FF, 1)
        down_rows = lax.dynamic_slice_in_dim(w_down, columns, MOE_FF, 0)
        gate_proj = jnp.dot(inputs, gate_cols, preferred_element_type=jnp.float32)
        up_proj = jnp.dot(inputs, up_cols, preferred_element_type=jnp.float32)
        activated = (jax.nn.silu(gate_proj) * up_proj).astype(jnp.bfloat16)
        projected = jnp.dot(activated, down_rows, preferred_element_type=jnp.float32)
        scaled = jnp.where(live, gate_of[picked], 0.0)[:, None] * projected
        return (carry.at[picked].add(scaled), None)
    moe, unused = lax.scan(one_expert, jnp.zeros((ROWS, D), jnp.float32), jnp.arange(EXPERTS, dtype=jnp.int32))
    return (hidden_f + moe).astype(jnp.bfloat16)
```

```python
import functools
import math

import jax
import jax.numpy as jnp
from jax import lax
from jax.experimental import pallas as pl
from jax.experimental.pallas import tpu as pltpu
from jax.sharding import PartitionSpec as P

MESH = pl.DeviceIdType.MESH
CORES = 2
TILE = 256

D = 2048
TOPK = 8
EXP_DEV = 2


epsilon = 1e-06


def attend(queries, new_kv, cache, lengths):
    row_count = queries.shape[0]
    kv_local = cache.shape[1]
    positions = cache.shape[2]
    head_dim = cache.shape[3] // 2
    group_size = queries.shape[1] // (head_dim * kv_local)
    query = queries.reshape(row_count, kv_local, group_size, head_dim)
    key_part = cache[..., :head_dim]
    value_part = cache[..., head_dim:]
    score_scale = 1.0 / math.sqrt(head_dim)
    scores = (
        jnp.einsum("rgqd,rgcd->rgqc", query, key_part, preferred_element_type=jnp.float32)
        * score_scale
    )
    fresh_score = (
        jnp.einsum(
            "rgqd,rgd->rgq", query, new_kv[..., :head_dim], preferred_element_type=jnp.float32
        )
        * score_scale
    )
    is_valid = (jnp.arange(positions, dtype=jnp.int32)[None, :] < lengths[:, None])[
        :, None, None, :
    ]
    masked = jnp.where(is_valid, scores, -1e30)
    row_max = jnp.maximum(jnp.max(masked, -1), fresh_score)
    exp_terms = jnp.where(is_valid, jnp.exp(masked - row_max[..., None]), 0.0)
    fresh_exp = jnp.exp(fresh_score - row_max)
    totals = jnp.sum(exp_terms, -1) + fresh_exp
    weights = (exp_terms / totals[..., None]).astype(jnp.bfloat16)
    fresh_weight = (fresh_exp / totals).astype(jnp.bfloat16)
    mixed = jnp.einsum("rgqc,rgcd->rgqd", weights, value_part, preferred_element_type=jnp.float32)
    mixed = mixed + fresh_weight.astype(jnp.float32)[..., None] * new_kv[
        :, :, None, head_dim:
    ].astype(jnp.float32)
    return mixed.astype(jnp.bfloat16).reshape(row_count, kv_local * group_size * head_dim)


def slot_tables(expert_ids, expert_gates, experts, capacity):
    route_weights = expert_gates / jnp.sum(expert_gates, 1, keepdims=True)
    matches = expert_ids[:, :, None] == jnp.arange(experts, dtype=jnp.int32)[None, None, :]
    chosen = jnp.any(matches, 1)
    slot_rank = jnp.cumsum(chosen.astype(jnp.int32), 0) - 1
    slot_map = chosen[None] & (
        slot_rank[None] == jnp.arange(capacity, dtype=jnp.int32)[:, None, None]
    )
    return (slot_map, slot_rank, route_weights)


def run_expert(gathered, w_gate, w_up, w_down):
    gate_proj = jnp.einsum("qcd,df->qcf", gathered, w_gate, preferred_element_type=jnp.float32)
    up_proj = jnp.einsum("qcd,df->qcf", gathered, w_up, preferred_element_type=jnp.float32)
    activated = (jax.nn.silu(gate_proj) * up_proj).astype(jnp.bfloat16)
    projected = jnp.einsum("qcf,fd->qcd", activated, w_down, preferred_element_type=jnp.float32)
    return lax.all_to_all(
        projected.astype(jnp.bfloat16), "ep", split_axis=0, concat_axis=0, tiled=True
    ).astype(projected.dtype)


def per_device(
    queries,
    new_kv,
    cache,
    lengths,
    out_weight,
    residual,
    norm_gain,
    expert_ids,
    expert_gates,
    w_gate,
    w_up,
    w_down,
):
    row_count = residual.shape[0]
    col_width = residual.shape[1]
    ep_size = lax.axis_size("ep")
    tp_size = lax.axis_size("tp")
    tp_rank = lax.axis_index("tp")
    experts = ep_size * EXP_DEV
    capacity = min(row_count, 2 * row_count * TOPK // experts)
    pieces = tp_size // EXP_DEV
    parity = tp_rank // pieces
    attn_local = attend(queries, new_kv, cache, lengths)
    attn_heads = lax.all_to_all(attn_local, "tp", split_axis=1, concat_axis=0, tiled=True)
    partial_value = jnp.dot(attn_heads, out_weight, preferred_element_type=jnp.float32)
    normed_full = None
    normed_share = None
    head_share = lax.psum_scatter(partial_value, "tp", scatter_dimension=1, tiled=True)
    hidden_share = (residual.astype(jnp.float32) + head_share).astype(jnp.bfloat16)
    hidden_f = hidden_share.astype(jnp.float32)
    squares = lax.psum(jnp.sum(hidden_f * hidden_f, 1, keepdims=True), "tp")
    inv_scale = lax.rsqrt(squares / D + epsilon)
    gain_share = lax.dynamic_slice_in_dim(norm_gain, tp_rank * col_width, col_width)
    normed_share = (hidden_f * inv_scale * gain_share).astype(jnp.bfloat16)
    slot_map, slot_rank, route_weights = slot_tables(expert_ids, expert_gates, experts, capacity)
    slot_grid = slot_map.reshape(capacity, row_count, ep_size, EXP_DEV)
    own_slots = lax.dynamic_index_in_dim(slot_grid, parity, 3, keepdims=False)
    normed_full = lax.all_gather(normed_share, "tp", axis=1, tiled=True)
    outgoing = jnp.einsum(
        "crq,rd->qcd",
        own_slots.astype(jnp.bfloat16),
        normed_full,
        preferred_element_type=jnp.float32,
    ).astype(jnp.bfloat16)
    returned = run_expert(
        lax.all_to_all(outgoing, "ep", split_axis=0, concat_axis=0, tiled=True),
        w_gate,
        w_up,
        w_down,
    )
    picked_rank = jnp.take_along_axis(slot_rank, expert_ids, 1)
    owner = expert_ids // EXP_DEV
    member = expert_ids % EXP_DEV
    flat = returned.reshape(ep_size * capacity, returned.shape[-1])
    index = owner * capacity + picked_rank
    weight = jnp.where(member == parity, route_weights, 0.0)
    moe_part = jnp.sum(weight[:, :, None] * flat[index], 1)
    moe_share = lax.psum_scatter(
        moe_part.astype(jnp.bfloat16), "tp", scatter_dimension=1, tiled=True
    ).astype(jnp.float32)
    return (hidden_share.astype(jnp.float32) + moe_share).astype(jnp.bfloat16)


def layer_kernel(
    ep_size,
    kvh,
    q_ref,
    new_ref,
    len_ref,
    resid_ref,
    gain_ref,
    ids_ref,
    gates_ref,
    cache_hbm,
    out_w_hbm,
    gate_hbm,
    up_hbm,
    down_hbm,
    out_ref,
    cache_v,
    out_w,
    w_gate,
    w_up,
    w_down,
    q_rows,
    o_rows,
    heads_out,
    heads,
    part_out,
    part_in,
    own_part,
    hidden,
    sq_out,
    sq_in,
    route,
    normed,
    activated,
    pair_keep,
    pair_out,
    pair_in,
    side_keep,
    side_out,
    side_in,
    line_out,
    line_in,
    load_sem,
    route_s,
    route_r,
    head_s,
    head_r,
    part_s,
    part_r,
    sq_s,
    sq_r,
    line_s,
    line_r,
    core_s,
    core_r,
    side_s,
    side_r,
    fwd_s,
    fwd_r,
    pair_s,
    pair_r,
    back_s,
    back_r,
    ret_s,
    ret_r,
):
    f32, bf16 = jnp.float32, jnp.bfloat16
    ep = lax.axis_index("ep")
    tp = lax.axis_index("tp")
    core = lax.rem(ep, CORES)
    line = lax.div(ep, CORES)
    chips = ep_size // CORES
    other_core = ep + 1 - 2 * core
    other_tp = 1 - tp
    rows_att = q_ref.shape[0]
    rows = resid_ref.shape[0]
    half = resid_ref.shape[1]
    width = 2 * half
    hd = new_ref.shape[2] // 2
    n_heads = q_ref.shape[1] // hd
    group = n_heads // kvh
    ctx = cache_v.shape[1] // kvh
    experts = route.shape[1]
    half_heads = n_heads // 2
    half_in = half_heads * hd
    hidden_units = w_down.shape[0]

    loads = [
        pltpu.make_async_copy(src, dst, load_sem.at[i])
        for i, (src, dst) in enumerate(
            (
                (cache_hbm, cache_v),
                (out_w_hbm, out_w),
                (gate_hbm, w_gate),
                (up_hbm, w_up),
                (down_hbm, w_down),
            )
        )
    ]
    for load in loads:
        load.start()

    barrier = pltpu.get_barrier_semaphore()
    for step in range(1, ep_size):
        pl.semaphore_signal(
            barrier,
            inc=1,
            device_id={"ep": lax.rem(ep + step, ep_size)},
            device_id_type=MESH,
        )
    pl.semaphore_signal(barrier, inc=1, device_id={"tp": other_tp}, device_id_type=MESH)

    def push(src, dst, send, recv, target):
        return pltpu.make_async_remote_copy(
            src_ref=src,
            dst_ref=dst,
            send_sem=send,
            recv_sem=recv,
            device_id=target,
            device_id_type=MESH,
        )

    sent = []

    gates = gates_ref[...]
    shares = gates / jnp.sum(gates, 1, keepdims=True)
    ids = ids_ref[...]
    lane = lax.broadcasted_iota(jnp.int32, (rows, 128), 1)
    dense = jnp.zeros((rows, 128), f32)
    for k in range(TOPK):
        dense = dense + jnp.where(ids[:, k : k + 1] == lane, shares[:, k : k + 1], 0.0)
    if rows < 128:
        dense = jnp.concatenate([dense, jnp.zeros((128 - rows, 128), f32)], 0)
    route[ep] = jnp.transpose(dense)[:experts]

    for h in range(0, n_heads, 8):
        by_head = jnp.stack([q_ref[:, i * hd : (i + 1) * hd].astype(f32) for i in range(h, h + 8)])
        q_rows[:, h : h + 8, :] = jnp.transpose(by_head, (1, 0, 2))

    scale = 1.0 / math.sqrt(hd)
    loads[0].wait()
    span = kvh * ctx
    head_id = lax.broadcasted_iota(jnp.int32, (n_heads, span), 0)
    slot_id = lax.broadcasted_iota(jnp.int32, (n_heads, span), 1)
    same_group = (head_id // group) == (slot_id // ctx)
    position = jnp.where(same_group, slot_id % ctx, ctx)

    def attend_row(r):
        q_f = q_rows[r]
        kv = cache_v[r]
        scores = (
            lax.dot_general(
                q_f.astype(bf16),
                kv[:, :hd],
                (((1,), (1,)), ((), ())),
                preferred_element_type=f32,
            )
            * scale
        )
        fresh_kv = new_ref[r].astype(f32)
        fresh_kv = jnp.broadcast_to(fresh_kv[:, None, :], (kvh, group, 2 * hd)).reshape(
            n_heads, 2 * hd
        )
        fresh = jnp.sum(q_f * fresh_kv[:, :hd], 1, keepdims=True) * scale
        valid = position < len_ref[r]
        masked = jnp.where(valid, scores, -1e30)
        top = jnp.maximum(jnp.max(masked, 1, keepdims=True), fresh)
        terms = jnp.where(valid, jnp.exp(masked - top), 0.0)
        fresh_term = jnp.exp(fresh - top)
        total = jnp.sum(terms, 1, keepdims=True) + fresh_term
        weights = (terms / total).astype(bf16)
        fresh_weight = (fresh_term / total).astype(bf16).astype(f32)
        mixed = jnp.dot(weights, kv[:, hd:], preferred_element_type=f32)
        mixed = mixed + fresh_weight * fresh_kv[:, hd:]
        o_rows[r] = mixed

    for r in range(rows_att):
        attend_row(r)

    pl.semaphore_wait(barrier, ep_size)

    def place_heads(owner, dst, at):
        for i in range(0, half_heads, 8):
            start = pl.multiple_of(owner * half_heads + i, 8)
            by_head = jnp.transpose(o_rows[:, pl.ds(start, 8), :], (1, 0, 2)).astype(bf16)
            for j in range(8):
                dst[at, (i + j) * hd : (i + j + 1) * hd] = by_head[j]

    place_heads(other_tp, heads_out, slice(None))
    my_rows = pl.ds(pl.multiple_of(tp * rows_att, rows_att), rows_att)
    head_copy = push(heads_out, heads.at[my_rows, :], head_s, head_r, {"tp": other_tp})
    head_copy.start()
    place_heads(tp, heads, my_rows)

    route_copies = []
    for step in range(1, ep_size):
        copy = push(
            route.at[ep],
            route.at[ep],
            route_s.at[step],
            route_r.at[step],
            {"ep": lax.rem(ep + step, ep_size)},
        )
        copy.start()
        route_copies.append(copy)

    loads[1].wait()
    head_copy.wait()

    chunks = part_out.shape[0]
    chunk = half // chunks
    part_copies = []
    for i in range(chunks):
        def project(j, carry, i=i):
            at = pl.multiple_of(j * TILE, TILE)
            cols = pl.ds(pl.multiple_of(other_tp * half + i * chunk + at, TILE), TILE)
            part_out[i, :, pl.ds(at, TILE)] = jnp.dot(
                heads[...], out_w[:, cols], preferred_element_type=f32
            ).astype(bf16)
            return carry

        lax.fori_loop(0, chunk // TILE, project, 0)
        copy = push(
            part_out.at[i], part_in.at[i], part_s.at[i], part_r.at[i], {"tp": other_tp}
        )
        copy.start()
        part_copies.append(copy)

    def project_own(j, carry):
        at = pl.multiple_of(j * TILE, TILE)
        cols = pl.ds(pl.multiple_of(tp * half + at, TILE), TILE)
        own_part[:, pl.ds(at, TILE)] = jnp.dot(
            heads[...], out_w[:, cols], preferred_element_type=f32
        ) + resid_ref[:, pl.ds(at, TILE)].astype(f32)
        return carry

    lax.fori_loop(0, half // TILE, project_own, 0)

    squares = jnp.zeros((rows, 1), f32)
    for i in range(chunks):
        part_copies[i].wait()
        cols = slice(i * chunk, (i + 1) * chunk)
        total = (own_part[:, cols] + part_in[i].astype(f32)).astype(bf16)
        hidden[:, cols] = total
        total = total.astype(f32)
        squares = squares + jnp.sum(total * total, 1, keepdims=True)
    sq_out[...] = jnp.broadcast_to(squares, sq_out.shape)
    sq_copy = push(sq_out, sq_in, sq_s, sq_r, {"tp": other_tp})
    sq_copy.start()
    my_cols = pl.ds(pl.multiple_of(tp * half, half), half)
    their_cols = pl.ds(pl.multiple_of(other_tp * half, half), half)
    gain = gain_ref[:, my_cols]
    sq_copy.wait()
    inv = lax.rsqrt((squares + sq_in[:, :1]) / width + epsilon)

    def block(chip, which, cols):
        return normed.at[pl.ds(pl.multiple_of((chip * CORES + which) * rows, rows), rows), cols]

    own_block = block(line, core, my_cols)
    own_block[...] = (hidden[...].astype(f32) * inv * gain).astype(bf16)

    lines = [None]
    for step in range(1, chips):
        copy = push(
            own_block,
            own_block,
            line_s.at[step],
            line_r.at[step],
            {"ep": lax.rem(line + step, chips) * CORES + core},
        )
        copy.start()
        lines.append(copy)
    sources = [lax.rem(line + chips - step, chips) for step in range(chips)]
    cores, sides, forwards = {}, {}, {}

    def spread(k):
        if k > 0:
            lines[k].wait_recv()
        here = block(sources[k], core, my_cols)
        sides[k] = push(here, here, side_s.at[k], side_r.at[k], {"tp": other_tp})
        sides[k].start()
        cores[k] = push(here, here, core_s.at[k], core_r.at[k], {"ep": other_core})
        cores[k].start()

    def forward(k):
        sides[k].wait_recv()
        there = block(sources[k], core, their_cols)
        forwards[k] = push(there, there, fwd_s.at[k], fwd_r.at[k], {"ep": other_core})
        forwards[k].start()

    pairs, backs, rets = {}, {}, {}
    expert = CORES * ep + tp

    def column(owner):
        row = route[owner, pl.ds(expert, 1), :]
        return jnp.transpose(jnp.broadcast_to(row, (128, 128)))[:rows, :1]

    def feed(k):
        cores[k].wait_recv()
        forwards[k].wait_recv()
        first = pl.multiple_of(sources[k] * (CORES * rows), CORES * rows)
        both = pl.ds(first, CORES * rows)

        def up_tile(j, carry):
            cols = pl.ds(pl.multiple_of(j * TILE, TILE), TILE)
            values = normed[both, :]
            gate_proj = jnp.dot(values, w_gate[:, cols], preferred_element_type=f32)
            up_proj = jnp.dot(values, w_up[:, cols], preferred_element_type=f32)
            silu = gate_proj / (1.0 + jnp.exp(-gate_proj))
            activated[:, cols] = (silu * up_proj).astype(bf16)
            return carry

        lax.fori_loop(0, hidden_units // TILE, up_tile, 0)
        kept = pl.ds(pl.multiple_of(core * rows, rows), rows)
        given = pl.ds(pl.multiple_of((1 - core) * rows, rows), rows)
        keep_weight = column(sources[k] * CORES + core)
        give_weight = column(sources[k] * CORES + 1 - core)

        def down_tile(j, carry):
            cols = pl.ds(pl.multiple_of(j * TILE, TILE), TILE)
            pair_out[k, :, cols] = (
                jnp.dot(activated[given, :], w_down[:, cols], preferred_element_type=f32)
                * give_weight
            ).astype(bf16)
            pair_keep[k, :, cols] = (
                jnp.dot(activated[kept, :], w_down[:, cols], preferred_element_type=f32)
                * keep_weight
            )
            return carry

        lax.fori_loop(0, width // TILE, down_tile, 0)
        pairs[k] = push(
            pair_out.at[k], pair_in.at[k], pair_s.at[k], pair_r.at[k], {"ep": other_core}
        )
        pairs[k].start()

    def cross(k):
        pairs[k].wait_recv()
        side_out[k] = (
            pair_keep[k, :, their_cols] + pair_in[k, :, their_cols].astype(f32)
        ).astype(bf16)
        backs[k] = push(
            side_out.at[k], side_in.at[k], back_s.at[k], back_r.at[k], {"tp": other_tp}
        )
        backs[k].start()
        side_keep[k] = pair_keep[k, :, my_cols] + pair_in[k, :, my_cols].astype(f32)

    def give_back(k):
        backs[k].wait_recv()
        total = side_keep[k] + side_in[k].astype(f32)
        if k == 0:
            side_keep[k] = total + hidden[...].astype(f32)
            return
        line_out[k] = total.astype(bf16)
        rets[k] = push(
            line_out.at[k],
            line_in.at[k],
            ret_s.at[k],
            ret_r.at[k],
            {"ep": sources[k] * CORES + core},
        )
        rets[k].start()

    spread(0)
    for copy in route_copies:
        copy.wait()
    for load in loads[2:]:
        load.wait()
    forward(0)
    for k in range(chips):
        if k + 1 < chips:
            spread(k + 1)
        feed(k)
        if k + 1 < chips:
            forward(k + 1)
        if k > 0:
            give_back(k - 1)
        cross(k)
    give_back(chips - 1)
    result = side_keep[0]
    for k in range(1, chips):
        rets[k].wait_recv()
        result = result + line_in[k].astype(f32)
    out_ref[...] = result.astype(bf16)
    for k in range(chips):
        cores[k].wait_send()
        sides[k].wait_send()
        forwards[k].wait_send()
        pairs[k].wait_send()
        backs[k].wait_send()
        if k > 0:
            lines[k].wait_send()
            rets[k].wait_send()


def fused(
    queries,
    new_kv,
    cache,
    lengths,
    out_weight,
    residual,
    norm_gain,
    expert_ids,
    expert_gates,
    w_gate,
    w_up,
    w_down,
):
    f32, bf16 = jnp.float32, jnp.bfloat16
    ep_size = lax.axis_size("ep")
    chips = ep_size // CORES
    rows_att, in_width = queries.shape
    kvh, ctx, kv_width = cache.shape[1:]
    hd = kv_width // 2
    group = in_width // (hd * kvh)
    rows, half = residual.shape
    width = 2 * half
    experts = ep_size * EXP_DEV
    chunks = 2
    vmem = pl.BlockSpec(memory_space=pltpu.VMEM)
    hbm = pl.BlockSpec(memory_space=pl.ANY)
    smem = pl.BlockSpec(memory_space=pltpu.SMEM)
    V = pltpu.VMEM
    dma = pltpu.SemaphoreType.DMA
    scratch = [
        V((rows_att, kvh * ctx, kv_width), bf16),
        V(out_weight.shape, bf16),
        V(w_gate.shape, bf16),
        V(w_up.shape, bf16),
        V(w_down.shape, bf16),
        V((rows_att, in_width // hd, hd), f32),
        V((rows_att, in_width // hd, hd), f32),
        V((rows_att, in_width // 2), bf16),
        V((rows, in_width // 2), bf16),
        V((chunks, rows, half // chunks), bf16),
        V((chunks, rows, half // chunks), bf16),
        V((rows, half), f32),
        V((rows, half), bf16),
        V((rows, 128), f32),
        V((rows, 128), f32),
        V((ep_size, experts, 128), f32),
        V((ep_size * rows, width), bf16),
        V((CORES * rows, w_down.shape[0]), bf16),
        V((chips, rows, width), f32),
        V((chips, rows, width), bf16),
        V((chips, rows, width), bf16),
        V((chips, rows, half), f32),
        V((chips, rows, half), bf16),
        V((chips, rows, half), bf16),
        V((chips, rows, half), bf16),
        V((chips, rows, half), bf16),
        dma((5,)),
        dma((ep_size,)),
        dma((ep_size,)),
        dma,
        dma,
        dma((chunks,)),
        dma((chunks,)),
        dma,
        dma,
    ] + [dma((chips,)) for _ in range(14)]
    return pl.pallas_call(
        functools.partial(layer_kernel, ep_size, kvh),
        out_shape=jax.ShapeDtypeStruct((rows, half), bf16),
        in_specs=[vmem, vmem, smem, vmem, vmem, vmem, vmem, hbm, hbm, hbm, hbm, hbm],
        out_specs=vmem,
        scratch_shapes=scratch,
        compiler_params=pltpu.CompilerParams(
            collective_id=0, has_side_effects=True, vmem_limit_bytes=56 * 1024 * 1024
        ),
    )(
        queries,
        new_kv,
        lengths,
        residual,
        norm_gain.reshape(1, width),
        expert_ids,
        expert_gates,
        cache.reshape(rows_att, kvh * ctx, kv_width),
        out_weight,
        w_gate,
        w_up,
        w_down,
    )


def solution(mesh):
    in_specs = (
        P(("groups", "ep", "tp"), None),
        P(("groups", "ep", "tp"), None, None),
        P(("groups", "ep", "tp"), None, None, None),
        P(("groups", "ep", "tp")),
        P("tp", None),
        P(("groups", "ep"), "tp"),
        P(),
        P(("groups", "ep"), None),
        P(("groups", "ep"), None),
        P(None, ("ep", "tp")),
        P(None, ("ep", "tp")),
        P(("ep", "tp"), None),
    )
    out_specs = P(("groups", "ep"), "tp")
    body = fused if mesh.shape["tp"] == EXP_DEV else per_device
    return jax.shard_map(
        body, mesh=mesh, in_specs=in_specs, out_specs=out_specs, check_vma=False
    )
```

```python
import functools
import math

import jax
import jax.numpy as jnp
from jax import lax
from jax.experimental import pallas as pl
from jax.experimental.pallas import tpu as pltpu
from jax.sharding import PartitionSpec as P

MESH = pl.DeviceIdType.MESH
CORES = 2
TILE = 256
BATCH = 4

D = 2048
TOPK = 8
EXP_DEV = 2


epsilon = 1e-06


def attend(queries, new_kv, cache, lengths):
    row_count = queries.shape[0]
    kv_local = cache.shape[1]
    positions = cache.shape[2]
    head_dim = cache.shape[3] // 2
    group_size = queries.shape[1] // (head_dim * kv_local)
    query = queries.reshape(row_count, kv_local, group_size, head_dim)
    key_part = cache[..., :head_dim]
    value_part = cache[..., head_dim:]
    score_scale = 1.0 / math.sqrt(head_dim)
    scores = (
        jnp.einsum("rgqd,rgcd->rgqc", query, key_part, preferred_element_type=jnp.float32)
        * score_scale
    )
    fresh_score = (
        jnp.einsum(
            "rgqd,rgd->rgq", query, new_kv[..., :head_dim], preferred_element_type=jnp.float32
        )
        * score_scale
    )
    is_valid = (jnp.arange(positions, dtype=jnp.int32)[None, :] < lengths[:, None])[
        :, None, None, :
    ]
    masked = jnp.where(is_valid, scores, -1e30)
    row_max = jnp.maximum(jnp.max(masked, -1), fresh_score)
    exp_terms = jnp.where(is_valid, jnp.exp(masked - row_max[..., None]), 0.0)
    fresh_exp = jnp.exp(fresh_score - row_max)
    totals = jnp.sum(exp_terms, -1) + fresh_exp
    weights = (exp_terms / totals[..., None]).astype(jnp.bfloat16)
    fresh_weight = (fresh_exp / totals).astype(jnp.bfloat16)
    mixed = jnp.einsum("rgqc,rgcd->rgqd", weights, value_part, preferred_element_type=jnp.float32)
    mixed = mixed + fresh_weight.astype(jnp.float32)[..., None] * new_kv[
        :, :, None, head_dim:
    ].astype(jnp.float32)
    return mixed.astype(jnp.bfloat16).reshape(row_count, kv_local * group_size * head_dim)


def slot_tables(expert_ids, expert_gates, experts, capacity):
    route_weights = expert_gates / jnp.sum(expert_gates, 1, keepdims=True)
    matches = expert_ids[:, :, None] == jnp.arange(experts, dtype=jnp.int32)[None, None, :]
    chosen = jnp.any(matches, 1)
    slot_rank = jnp.cumsum(chosen.astype(jnp.int32), 0) - 1
    slot_map = chosen[None] & (
        slot_rank[None] == jnp.arange(capacity, dtype=jnp.int32)[:, None, None]
    )
    return (slot_map, slot_rank, route_weights)


def run_expert(gathered, w_gate, w_up, w_down):
    gate_proj = jnp.einsum("qcd,df->qcf", gathered, w_gate, preferred_element_type=jnp.float32)
    up_proj = jnp.einsum("qcd,df->qcf", gathered, w_up, preferred_element_type=jnp.float32)
    activated = (jax.nn.silu(gate_proj) * up_proj).astype(jnp.bfloat16)
    projected = jnp.einsum("qcf,fd->qcd", activated, w_down, preferred_element_type=jnp.float32)
    return lax.all_to_all(
        projected.astype(jnp.bfloat16), "ep", split_axis=0, concat_axis=0, tiled=True
    ).astype(projected.dtype)


def per_device(
    queries,
    new_kv,
    cache,
    lengths,
    out_weight,
    residual,
    norm_gain,
    expert_ids,
    expert_gates,
    w_gate,
    w_up,
    w_down,
):
    row_count = residual.shape[0]
    col_width = residual.shape[1]
    ep_size = lax.axis_size("ep")
    tp_size = lax.axis_size("tp")
    tp_rank = lax.axis_index("tp")
    experts = ep_size * EXP_DEV
    capacity = min(row_count, 2 * row_count * TOPK // experts)
    pieces = tp_size // EXP_DEV
    parity = tp_rank // pieces
    attn_local = attend(queries, new_kv, cache, lengths)
    attn_heads = lax.all_to_all(attn_local, "tp", split_axis=1, concat_axis=0, tiled=True)
    partial_value = jnp.dot(attn_heads, out_weight, preferred_element_type=jnp.float32)
    normed_full = None
    normed_share = None
    head_share = lax.psum_scatter(partial_value, "tp", scatter_dimension=1, tiled=True)
    hidden_share = (residual.astype(jnp.float32) + head_share).astype(jnp.bfloat16)
    hidden_f = hidden_share.astype(jnp.float32)
    squares = lax.psum(jnp.sum(hidden_f * hidden_f, 1, keepdims=True), "tp")
    inv_scale = lax.rsqrt(squares / D + epsilon)
    gain_share = lax.dynamic_slice_in_dim(norm_gain, tp_rank * col_width, col_width)
    normed_share = (hidden_f * inv_scale * gain_share).astype(jnp.bfloat16)
    slot_map, slot_rank, route_weights = slot_tables(expert_ids, expert_gates, experts, capacity)
    slot_grid = slot_map.reshape(capacity, row_count, ep_size, EXP_DEV)
    own_slots = lax.dynamic_index_in_dim(slot_grid, parity, 3, keepdims=False)
    normed_full = lax.all_gather(normed_share, "tp", axis=1, tiled=True)
    outgoing = jnp.einsum(
        "crq,rd->qcd",
        own_slots.astype(jnp.bfloat16),
        normed_full,
        preferred_element_type=jnp.float32,
    ).astype(jnp.bfloat16)
    returned = run_expert(
        lax.all_to_all(outgoing, "ep", split_axis=0, concat_axis=0, tiled=True),
        w_gate,
        w_up,
        w_down,
    )
    picked_rank = jnp.take_along_axis(slot_rank, expert_ids, 1)
    owner = expert_ids // EXP_DEV
    member = expert_ids % EXP_DEV
    flat = returned.reshape(ep_size * capacity, returned.shape[-1])
    index = owner * capacity + picked_rank
    weight = jnp.where(member == parity, route_weights, 0.0)
    moe_part = jnp.sum(weight[:, :, None] * flat[index], 1)
    moe_share = lax.psum_scatter(
        moe_part.astype(jnp.bfloat16), "tp", scatter_dimension=1, tiled=True
    ).astype(jnp.float32)
    return (hidden_share.astype(jnp.float32) + moe_share).astype(jnp.bfloat16)


def layer_kernel(
    ep_size,
    kvh,
    q_ref,
    new_ref,
    len_ref,
    resid_ref,
    gain_ref,
    ids_ref,
    gates_ref,
    cache_hbm,
    out_w_hbm,
    gate_hbm,
    up_hbm,
    down_hbm,
    out_ref,
    cache_v,
    out_w,
    w_gate,
    w_up,
    w_down,
    q_rows,
    o_rows,
    heads_out,
    heads,
    part_out,
    part_in,
    own_part,
    hidden,
    sq_out,
    sq_in,
    route,
    normed,
    activated,
    pair_keep,
    pair_out,
    pair_in,
    side_keep,
    side_out,
    side_in,
    line_out,
    line_in,
    load_sem,
    route_s,
    route_r,
    head_s,
    head_r,
    part_s,
    part_r,
    sq_s,
    sq_r,
    line_s,
    line_r,
    core_s,
    core_r,
    side_s,
    side_r,
    fwd_s,
    fwd_r,
    pair_s,
    pair_r,
    back_s,
    back_r,
    ret_s,
    ret_r,
):
    f32, bf16 = jnp.float32, jnp.bfloat16
    ep = lax.axis_index("ep")
    tp = lax.axis_index("tp")
    core = lax.rem(ep, CORES)
    line = lax.div(ep, CORES)
    chips = ep_size // CORES
    other_core = ep + 1 - 2 * core
    other_tp = 1 - tp
    rows_att = q_ref.shape[0]
    rows = resid_ref.shape[0]
    half = resid_ref.shape[1]
    width = 2 * half
    hd = new_ref.shape[2] // 2
    n_heads = q_ref.shape[1] // hd
    group = n_heads // kvh
    ctx = cache_v.shape[1] // kvh
    experts = route.shape[1]
    half_heads = n_heads // 2
    half_in = half_heads * hd
    hidden_units = w_down.shape[0]

    loads = [
        pltpu.make_async_copy(src, dst, load_sem.at[i])
        for i, (src, dst) in enumerate(
            (
                (cache_hbm, cache_v),
                (out_w_hbm, out_w),
                (gate_hbm, w_gate),
                (up_hbm, w_up),
                (down_hbm, w_down),
            )
        )
    ]
    for load in loads:
        load.start()

    barrier = pltpu.get_barrier_semaphore()
    for step in range(1, ep_size):
        pl.semaphore_signal(
            barrier,
            inc=1,
            device_id={"ep": lax.rem(ep + step, ep_size)},
            device_id_type=MESH,
        )
    pl.semaphore_signal(barrier, inc=1, device_id={"tp": other_tp}, device_id_type=MESH)

    def push(src, dst, send, recv, target):
        return pltpu.make_async_remote_copy(
            src_ref=src,
            dst_ref=dst,
            send_sem=send,
            recv_sem=recv,
            device_id=target,
            device_id_type=MESH,
        )

    sent = []

    gates = gates_ref[...]
    shares = gates / jnp.sum(gates, 0, keepdims=True)
    ids = ids_ref[...]
    expert_id = lax.broadcasted_iota(jnp.int32, (experts, rows), 0)
    dense = jnp.zeros((experts, rows), f32)
    for k in range(TOPK):
        dense = dense + jnp.where(ids[k : k + 1] == expert_id, shares[k : k + 1], 0.0)
    if rows < 128:
        dense = jnp.concatenate([dense, jnp.zeros((experts, 128 - rows), f32)], 1)
    route[ep] = dense

    for h in range(0, n_heads, 8):
        by_head = jnp.stack([q_ref[:, i * hd : (i + 1) * hd].astype(f32) for i in range(h, h + 8)])
        q_rows[:, h : h + 8, :] = jnp.transpose(by_head, (1, 0, 2))

    scale = 1.0 / math.sqrt(hd)
    loads[0].wait()
    span = kvh * ctx
    tall = BATCH * n_heads
    head_id = lax.broadcasted_iota(jnp.int32, (n_heads, span), 0)
    slot_id = lax.broadcasted_iota(jnp.int32, (n_heads, span), 1)
    same_group = (head_id // group) == (slot_id // ctx)
    position = jnp.where(same_group, slot_id % ctx, ctx)

    def attend_rows(first):
        q_f = q_rows[first : first + BATCH].reshape(tall, hd)
        q_b = q_f.astype(bf16)
        each = range(BATCH)
        kv = [cache_v[first + i] for i in each]
        scores = jnp.concatenate(
            [
                lax.dot_general(
                    q_b[i * n_heads : (i + 1) * n_heads],
                    kv[i][:, :hd],
                    (((1,), (1,)), ((), ())),
                    preferred_element_type=f32,
                )
                for i in each
            ],
            0,
        )
        scores = scores * scale
        fresh_kv = jnp.concatenate(
            [
                jnp.broadcast_to(
                    new_ref[first + i].astype(f32)[:, None, :], (kvh, group, 2 * hd)
                ).reshape(n_heads, 2 * hd)
                for i in each
            ],
            0,
        )
        fresh = jnp.sum(q_f * fresh_kv[:, :hd], 1, keepdims=True) * scale
        valid = jnp.concatenate(
            [jnp.where(position < len_ref[first + i], 1.0, 0.0) for i in each], 0
        ) > 0.5
        masked = jnp.where(valid, scores, -1e30)
        top = jnp.maximum(jnp.max(masked, 1, keepdims=True), fresh)
        terms = jnp.where(valid, jnp.exp(masked - top), 0.0)
        fresh_term = jnp.exp(fresh - top)
        total = jnp.sum(terms, 1, keepdims=True) + fresh_term
        weights = (terms / total).astype(bf16)
        fresh_weight = (fresh_term / total).astype(bf16).astype(f32)
        mixed = jnp.concatenate(
            [
                jnp.dot(
                    weights[i * n_heads : (i + 1) * n_heads],
                    kv[i][:, hd:],
                    preferred_element_type=f32,
                )
                for i in each
            ],
            0,
        )
        mixed = mixed + fresh_weight * fresh_kv[:, hd:]
        o_rows[first : first + BATCH] = mixed.reshape(BATCH, n_heads, hd)

    part = rows_att // 2

    def place_heads(owner, first, dst, at):
        for i in range(0, half_heads, 8):
            start = pl.multiple_of(owner * half_heads + i, 8)
            by_head = jnp.transpose(o_rows[first : first + part, pl.ds(start, 8), :], (1, 0, 2))
            by_head = by_head.astype(bf16)
            for j in range(8):
                dst[at, (i + j) * hd : (i + j + 1) * hd] = by_head[j]

    head_copies = []
    for p in range(2):
        for first in range(p * part, (p + 1) * part, BATCH):
            attend_rows(first)
        if p == 0:
            pl.semaphore_wait(barrier, ep_size)
        here = pl.ds(p * part, part)
        there = pl.ds(pl.multiple_of(tp * rows_att + p * part, part), part)
        place_heads(other_tp, p * part, heads_out, here)
        copy = push(
            heads_out.at[here, :], heads.at[there, :], head_s.at[p], head_r.at[p], {"tp": other_tp}
        )
        copy.start()
        head_copies.append(copy)
        place_heads(tp, p * part, heads, there)

    route_copies = []
    for step in range(1, ep_size):
        copy = push(
            route.at[ep],
            route.at[ep],
            route_s.at[step],
            route_r.at[step],
            {"ep": lax.rem(ep + step, ep_size)},
        )
        copy.start()
        route_copies.append(copy)

    loads[1].wait()
    for copy in head_copies:
        copy.wait()

    chunks = part_out.shape[0]
    chunk = half // chunks
    part_copies = []
    for i in range(chunks):
        def project(j, carry, i=i):
            at = pl.multiple_of(j * TILE, TILE)
            cols = pl.ds(pl.multiple_of(other_tp * half + i * chunk + at, TILE), TILE)
            part_out[i, :, pl.ds(at, TILE)] = jnp.dot(
                heads[...], out_w[:, cols], preferred_element_type=f32
            ).astype(bf16)
            return carry

        lax.fori_loop(0, chunk // TILE, project, 0)
        copy = push(
            part_out.at[i], part_in.at[i], part_s.at[i], part_r.at[i], {"tp": other_tp}
        )
        copy.start()
        part_copies.append(copy)

    def project_own(j, carry):
        at = pl.multiple_of(j * TILE, TILE)
        cols = pl.ds(pl.multiple_of(tp * half + at, TILE), TILE)
        own_part[:, pl.ds(at, TILE)] = jnp.dot(
            heads[...], out_w[:, cols], preferred_element_type=f32
        ) + resid_ref[:, pl.ds(at, TILE)].astype(f32)
        return carry

    lax.fori_loop(0, half // TILE, project_own, 0)

    squares = jnp.zeros((rows, 1), f32)
    for i in range(chunks):
        part_copies[i].wait()
        cols = slice(i * chunk, (i + 1) * chunk)
        total = (own_part[:, cols] + part_in[i].astype(f32)).astype(bf16)
        hidden[:, cols] = total
        total = total.astype(f32)
        squares = squares + jnp.sum(total * total, 1, keepdims=True)
    sq_out[...] = jnp.broadcast_to(squares, sq_out.shape)
    sq_copy = push(sq_out, sq_in, sq_s, sq_r, {"tp": other_tp})
    sq_copy.start()
    my_cols = pl.ds(pl.multiple_of(tp * half, half), half)
    their_cols = pl.ds(pl.multiple_of(other_tp * half, half), half)
    gain = gain_ref[:, my_cols]
    sq_copy.wait()
    inv = lax.rsqrt((squares + sq_in[:, :1]) / width + epsilon)

    def block(chip, which, cols):
        return normed.at[pl.ds(pl.multiple_of((chip * CORES + which) * rows, rows), rows), cols]

    own_block = block(line, core, my_cols)
    own_block[...] = (hidden[...].astype(f32) * inv * gain).astype(bf16)

    lines = [None]
    for step in range(1, chips):
        copy = push(
            own_block,
            own_block,
            line_s.at[step],
            line_r.at[step],
            {"ep": lax.rem(line + step, chips) * CORES + core},
        )
        copy.start()
        lines.append(copy)
    sources = [lax.rem(line + chips - step, chips) for step in range(chips)]
    cores, sides, forwards = {}, {}, {}

    def spread(k):
        if k > 0:
            lines[k].wait_recv()
        here = block(sources[k], core, my_cols)
        sides[k] = push(here, here, side_s.at[k], side_r.at[k], {"tp": other_tp})
        sides[k].start()
        cores[k] = push(here, here, core_s.at[k], core_r.at[k], {"ep": other_core})
        cores[k].start()

    def forward(k):
        sides[k].wait_recv()
        there = block(sources[k], core, their_cols)
        forwards[k] = push(there, there, fwd_s.at[k], fwd_r.at[k], {"ep": other_core})
        forwards[k].start()

    pairs, backs, rets = {}, {}, {}
    expert = CORES * ep + tp

    def column(owner):
        row = route[owner, pl.ds(expert, 1), :]
        return jnp.transpose(jnp.broadcast_to(row, (128, 128)))[:rows, :1]

    low = pl.ds(pl.multiple_of((1 - core) * rows, rows), rows)
    high = pl.ds(pl.multiple_of(core * rows, rows), rows)

    def feed(k):
        cores[k].wait_recv()
        forwards[k].wait_recv()
        first = pl.multiple_of(sources[k] * (CORES * rows), CORES * rows)
        both = pl.ds(first, CORES * rows)

        def up_tile(j, carry):
            cols = pl.ds(pl.multiple_of(j * TILE, TILE), TILE)
            values = normed[both, :]
            gate_proj = jnp.dot(values, w_gate[:, cols], preferred_element_type=f32)
            up_proj = jnp.dot(values, w_up[:, cols], preferred_element_type=f32)
            silu = gate_proj / (1.0 + jnp.exp(-gate_proj))
            both_rows = (silu * up_proj).astype(bf16)
            activated[low, cols] = both_rows[:rows]
            activated[high, cols] = both_rows[rows:]
            return carry

        lax.fori_loop(0, hidden_units // TILE, up_tile, 0)
        keep_weight = column(sources[k] * CORES + core)
        give_weight = column(sources[k] * CORES + 1 - core)

        for h, owner in enumerate((other_tp, tp)):
            def down_tile(j, carry, h=h, owner=owner):
                at = pl.multiple_of(j * TILE, TILE)
                cols = pl.ds(pl.multiple_of(owner * half + at, TILE), TILE)
                value = jnp.dot(activated[...], w_down[:, cols], preferred_element_type=f32)
                pair_out[k, h, :, pl.ds(at, TILE)] = (value[:rows] * give_weight).astype(bf16)
                pair_keep[k, h, :, pl.ds(at, TILE)] = value[rows:] * keep_weight
                return carry

            lax.fori_loop(0, half // TILE, down_tile, 0)
            pairs[k, h] = push(
                pair_out.at[k, h],
                pair_in.at[k, h],
                pair_s.at[k, h],
                pair_r.at[k, h],
                {"ep": other_core},
            )
            pairs[k, h].start()

    def cross(k):
        pairs[k, 0].wait_recv()
        side_out[k] = (pair_keep[k, 0] + pair_in[k, 0].astype(f32)).astype(bf16)
        backs[k] = push(
            side_out.at[k], side_in.at[k], back_s.at[k], back_r.at[k], {"tp": other_tp}
        )
        backs[k].start()
        pairs[k, 1].wait_recv()
        side_keep[k] = pair_keep[k, 1] + pair_in[k, 1].astype(f32)

    def give_back(k):
        backs[k].wait_recv()
        total = side_keep[k] + side_in[k].astype(f32)
        if k == 0:
            side_keep[k] = total + hidden[...].astype(f32)
            return
        line_out[k] = total.astype(bf16)
        rets[k] = push(
            line_out.at[k],
            line_in.at[k],
            ret_s.at[k],
            ret_r.at[k],
            {"ep": sources[k] * CORES + core},
        )
        rets[k].start()

    spread(0)
    for copy in route_copies:
        copy.wait()
    for load in loads[2:]:
        load.wait()
    forward(0)
    for k in range(chips):
        if k + 1 < chips:
            spread(k + 1)
        feed(k)
        if k + 1 < chips:
            forward(k + 1)
        if k > 0:
            give_back(k - 1)
        cross(k)
    give_back(chips - 1)
    result = side_keep[0]
    for k in range(1, chips):
        rets[k].wait_recv()
        result = result + line_in[k].astype(f32)
    out_ref[...] = result.astype(bf16)
    for k in range(chips):
        cores[k].wait_send()
        sides[k].wait_send()
        forwards[k].wait_send()
        pairs[k, 0].wait_send()
        pairs[k, 1].wait_send()
        backs[k].wait_send()
        if k > 0:
            lines[k].wait_send()
            rets[k].wait_send()


def fused(
    queries,
    new_kv,
    cache,
    lengths,
    out_weight,
    residual,
    norm_gain,
    expert_ids,
    expert_gates,
    w_gate,
    w_up,
    w_down,
):
    f32, bf16 = jnp.float32, jnp.bfloat16
    ep_size = lax.axis_size("ep")
    chips = ep_size // CORES
    rows_att, in_width = queries.shape
    kvh, ctx, kv_width = cache.shape[1:]
    hd = kv_width // 2
    group = in_width // (hd * kvh)
    rows, half = residual.shape
    width = 2 * half
    experts = ep_size * EXP_DEV
    chunks = 2
    vmem = pl.BlockSpec(memory_space=pltpu.VMEM)
    hbm = pl.BlockSpec(memory_space=pl.ANY)
    smem = pl.BlockSpec(memory_space=pltpu.SMEM)
    V = pltpu.VMEM
    dma = pltpu.SemaphoreType.DMA
    scratch = [
        V((rows_att, kvh * ctx, kv_width), bf16),
        V(out_weight.shape, bf16),
        V(w_gate.shape, bf16),
        V(w_up.shape, bf16),
        V(w_down.shape, bf16),
        V((rows_att, in_width // hd, hd), f32),
        V((rows_att, in_width // hd, hd), f32),
        V((rows_att, in_width // 2), bf16),
        V((rows, in_width // 2), bf16),
        V((chunks, rows, half // chunks), bf16),
        V((chunks, rows, half // chunks), bf16),
        V((rows, half), f32),
        V((rows, half), bf16),
        V((rows, 128), f32),
        V((rows, 128), f32),
        V((ep_size, experts, 128), f32),
        V((ep_size * rows, width), bf16),
        V((CORES * rows, w_down.shape[0]), bf16),
        V((chips, 2, rows, half), f32),
        V((chips, 2, rows, half), bf16),
        V((chips, 2, rows, half), bf16),
        V((chips, rows, half), f32),
        V((chips, rows, half), bf16),
        V((chips, rows, half), bf16),
        V((chips, rows, half), bf16),
        V((chips, rows, half), bf16),
        dma((5,)),
        dma((ep_size,)),
        dma((ep_size,)),
        dma((2,)),
        dma((2,)),
        dma((chunks,)),
        dma((chunks,)),
        dma,
        dma,
    ] + [dma((chips,)) for _ in range(8)] + [dma((chips, 2))] * 2 + [dma((chips,)) for _ in range(4)]
    return pl.pallas_call(
        functools.partial(layer_kernel, ep_size, kvh),
        out_shape=jax.ShapeDtypeStruct((rows, half), bf16),
        in_specs=[vmem, vmem, smem, vmem, vmem, vmem, vmem, hbm, hbm, hbm, hbm, hbm],
        out_specs=vmem,
        scratch_shapes=scratch,
        compiler_params=pltpu.CompilerParams(
            collective_id=0, has_side_effects=True, vmem_limit_bytes=56 * 1024 * 1024
        ),
    )(
        queries,
        new_kv,
        lengths,
        residual,
        norm_gain.reshape(1, width),
        expert_ids.T,
        expert_gates.T,
        cache.reshape(rows_att, kvh * ctx, kv_width),
        out_weight,
        w_gate,
        w_up,
        w_down,
    )


def solution(mesh):
    in_specs = (
        P(("groups", "ep", "tp"), None),
        P(("groups", "ep", "tp"), None, None),
        P(("groups", "ep", "tp"), None, None, None),
        P(("groups", "ep", "tp")),
        P("tp", None),
        P(("groups", "ep"), "tp"),
        P(),
        P(("groups", "ep"), None),
        P(("groups", "ep"), None),
        P(None, ("ep", "tp")),
        P(None, ("ep", "tp")),
        P(("ep", "tp"), None),
    )
    out_specs = P(("groups", "ep"), "tp")
    body = fused if mesh.shape["tp"] == EXP_DEV else per_device
    return jax.shard_map(
        body, mesh=mesh, in_specs=in_specs, out_specs=out_specs, check_vma=False
    )
```

```python
import functools
import math

import jax
import jax.numpy as jnp
from jax import lax
from jax.experimental import pallas as pl
from jax.experimental.pallas import tpu as pltpu
from jax.sharding import PartitionSpec as P

MESH = pl.DeviceIdType.MESH
CORES = 2
TILE = 256
BATCH = 4

D = 2048
TOPK = 8
EXP_DEV = 2


epsilon = 1e-06


def attend(queries, new_kv, cache, lengths):
    row_count = queries.shape[0]
    kv_local = cache.shape[1]
    positions = cache.shape[2]
    head_dim = cache.shape[3] // 2
    group_size = queries.shape[1] // (head_dim * kv_local)
    query = queries.reshape(row_count, kv_local, group_size, head_dim)
    key_part = cache[..., :head_dim]
    value_part = cache[..., head_dim:]
    score_scale = 1.0 / math.sqrt(head_dim)
    scores = (
        jnp.einsum("rgqd,rgcd->rgqc", query, key_part, preferred_element_type=jnp.float32)
        * score_scale
    )
    fresh_score = (
        jnp.einsum(
            "rgqd,rgd->rgq", query, new_kv[..., :head_dim], preferred_element_type=jnp.float32
        )
        * score_scale
    )
    is_valid = (jnp.arange(positions, dtype=jnp.int32)[None, :] < lengths[:, None])[
        :, None, None, :
    ]
    masked = jnp.where(is_valid, scores, -1e30)
    row_max = jnp.maximum(jnp.max(masked, -1), fresh_score)
    exp_terms = jnp.where(is_valid, jnp.exp(masked - row_max[..., None]), 0.0)
    fresh_exp = jnp.exp(fresh_score - row_max)
    totals = jnp.sum(exp_terms, -1) + fresh_exp
    weights = (exp_terms / totals[..., None]).astype(jnp.bfloat16)
    fresh_weight = (fresh_exp / totals).astype(jnp.bfloat16)
    mixed = jnp.einsum("rgqc,rgcd->rgqd", weights, value_part, preferred_element_type=jnp.float32)
    mixed = mixed + fresh_weight.astype(jnp.float32)[..., None] * new_kv[
        :, :, None, head_dim:
    ].astype(jnp.float32)
    return mixed.astype(jnp.bfloat16).reshape(row_count, kv_local * group_size * head_dim)


def slot_tables(expert_ids, expert_gates, experts, capacity):
    route_weights = expert_gates / jnp.sum(expert_gates, 1, keepdims=True)
    matches = expert_ids[:, :, None] == jnp.arange(experts, dtype=jnp.int32)[None, None, :]
    chosen = jnp.any(matches, 1)
    slot_rank = jnp.cumsum(chosen.astype(jnp.int32), 0) - 1
    slot_map = chosen[None] & (
        slot_rank[None] == jnp.arange(capacity, dtype=jnp.int32)[:, None, None]
    )
    return (slot_map, slot_rank, route_weights)


def run_expert(gathered, w_gate, w_up, w_down):
    gate_proj = jnp.einsum("qcd,df->qcf", gathered, w_gate, preferred_element_type=jnp.float32)
    up_proj = jnp.einsum("qcd,df->qcf", gathered, w_up, preferred_element_type=jnp.float32)
    activated = (jax.nn.silu(gate_proj) * up_proj).astype(jnp.bfloat16)
    projected = jnp.einsum("qcf,fd->qcd", activated, w_down, preferred_element_type=jnp.float32)
    return lax.all_to_all(
        projected.astype(jnp.bfloat16), "ep", split_axis=0, concat_axis=0, tiled=True
    ).astype(projected.dtype)


def per_device(
    queries,
    new_kv,
    cache,
    lengths,
    out_weight,
    residual,
    norm_gain,
    expert_ids,
    expert_gates,
    w_gate,
    w_up,
    w_down,
):
    row_count = residual.shape[0]
    col_width = residual.shape[1]
    ep_size = lax.axis_size("ep")
    tp_size = lax.axis_size("tp")
    tp_rank = lax.axis_index("tp")
    experts = ep_size * EXP_DEV
    capacity = min(row_count, 2 * row_count * TOPK // experts)
    pieces = tp_size // EXP_DEV
    parity = tp_rank // pieces
    attn_local = attend(queries, new_kv, cache, lengths)
    attn_heads = lax.all_to_all(attn_local, "tp", split_axis=1, concat_axis=0, tiled=True)
    partial_value = jnp.dot(attn_heads, out_weight, preferred_element_type=jnp.float32)
    normed_full = None
    normed_share = None
    head_share = lax.psum_scatter(partial_value, "tp", scatter_dimension=1, tiled=True)
    hidden_share = (residual.astype(jnp.float32) + head_share).astype(jnp.bfloat16)
    hidden_f = hidden_share.astype(jnp.float32)
    squares = lax.psum(jnp.sum(hidden_f * hidden_f, 1, keepdims=True), "tp")
    inv_scale = lax.rsqrt(squares / D + epsilon)
    gain_share = lax.dynamic_slice_in_dim(norm_gain, tp_rank * col_width, col_width)
    normed_share = (hidden_f * inv_scale * gain_share).astype(jnp.bfloat16)
    slot_map, slot_rank, route_weights = slot_tables(expert_ids, expert_gates, experts, capacity)
    slot_grid = slot_map.reshape(capacity, row_count, ep_size, EXP_DEV)
    own_slots = lax.dynamic_index_in_dim(slot_grid, parity, 3, keepdims=False)
    normed_full = lax.all_gather(normed_share, "tp", axis=1, tiled=True)
    outgoing = jnp.einsum(
        "crq,rd->qcd",
        own_slots.astype(jnp.bfloat16),
        normed_full,
        preferred_element_type=jnp.float32,
    ).astype(jnp.bfloat16)
    returned = run_expert(
        lax.all_to_all(outgoing, "ep", split_axis=0, concat_axis=0, tiled=True),
        w_gate,
        w_up,
        w_down,
    )
    picked_rank = jnp.take_along_axis(slot_rank, expert_ids, 1)
    owner = expert_ids // EXP_DEV
    member = expert_ids % EXP_DEV
    flat = returned.reshape(ep_size * capacity, returned.shape[-1])
    index = owner * capacity + picked_rank
    weight = jnp.where(member == parity, route_weights, 0.0)
    moe_part = jnp.sum(weight[:, :, None] * flat[index], 1)
    moe_share = lax.psum_scatter(
        moe_part.astype(jnp.bfloat16), "tp", scatter_dimension=1, tiled=True
    ).astype(jnp.float32)
    return (hidden_share.astype(jnp.float32) + moe_share).astype(jnp.bfloat16)


def layer_kernel(
    ep_size,
    kvh,
    q_ref,
    new_ref,
    len_ref,
    resid_ref,
    gain_ref,
    ids_ref,
    gates_ref,
    cache_hbm,
    out_w_hbm,
    gate_hbm,
    up_hbm,
    down_hbm,
    out_ref,
    cache_v,
    out_w,
    w_gate,
    w_up,
    w_down,
    q_rows,
    o_rows,
    heads_out,
    heads,
    part_out,
    part_in,
    own_part,
    hidden,
    sq_out,
    sq_in,
    inv_rows,
    route,
    normed,
    activated,
    pair_keep,
    pair_out,
    pair_in,
    side_keep,
    side_out,
    side_in,
    line_out,
    line_in,
    load_sem,
    route_s,
    route_r,
    head_s,
    head_r,
    part_s,
    part_r,
    sq_s,
    sq_r,
    inv_s,
    inv_r,
    line_s,
    line_r,
    core_s,
    core_r,
    side_s,
    side_r,
    fwd_s,
    fwd_r,
    pair_s,
    pair_r,
    back_s,
    back_r,
    ret_s,
    ret_r,
):
    f32, bf16 = jnp.float32, jnp.bfloat16
    ep = lax.axis_index("ep")
    tp = lax.axis_index("tp")
    core = lax.rem(ep, CORES)
    line = lax.div(ep, CORES)
    chips = ep_size // CORES
    other_core = ep + 1 - 2 * core
    other_tp = 1 - tp
    rows_att = q_ref.shape[0]
    rows = resid_ref.shape[0]
    half = resid_ref.shape[1]
    width = 2 * half
    hd = new_ref.shape[2] // 2
    n_heads = q_ref.shape[1] // hd
    group = n_heads // kvh
    ctx = cache_v.shape[1] // kvh
    experts = route.shape[1]
    half_heads = n_heads // 2
    half_in = half_heads * hd
    hidden_units = w_down.shape[0]

    loads = [
        pltpu.make_async_copy(src, dst, load_sem.at[i])
        for i, (src, dst) in enumerate(
            (
                (cache_hbm, cache_v),
                (out_w_hbm, out_w),
                (gate_hbm, w_gate),
                (up_hbm, w_up),
                (down_hbm, w_down),
            )
        )
    ]
    for load in loads:
        load.start()

    barrier = pltpu.get_barrier_semaphore()
    for step in range(1, ep_size):
        pl.semaphore_signal(
            barrier,
            inc=1,
            device_id={"ep": lax.rem(ep + step, ep_size)},
            device_id_type=MESH,
        )
    pl.semaphore_signal(barrier, inc=1, device_id={"tp": other_tp}, device_id_type=MESH)

    def push(src, dst, send, recv, target):
        return pltpu.make_async_remote_copy(
            src_ref=src,
            dst_ref=dst,
            send_sem=send,
            recv_sem=recv,
            device_id=target,
            device_id_type=MESH,
        )

    sent = []

    gates = gates_ref[...]
    shares = gates / jnp.sum(gates, 0, keepdims=True)
    ids = ids_ref[...]
    expert_id = lax.broadcasted_iota(jnp.int32, (experts, rows), 0)
    dense = jnp.zeros((experts, rows), f32)
    for k in range(TOPK):
        dense = dense + jnp.where(ids[k : k + 1] == expert_id, shares[k : k + 1], 0.0)
    if rows < 128:
        dense = jnp.concatenate([dense, jnp.zeros((experts, 128 - rows), f32)], 1)
    route[ep] = dense

    for h in range(0, n_heads, 8):
        by_head = jnp.stack([q_ref[:, i * hd : (i + 1) * hd].astype(f32) for i in range(h, h + 8)])
        q_rows[:, h : h + 8, :] = jnp.transpose(by_head, (1, 0, 2))

    scale = 1.0 / math.sqrt(hd)
    loads[0].wait()
    span = kvh * ctx
    tall = BATCH * n_heads
    head_id = lax.broadcasted_iota(jnp.int32, (n_heads, span), 0)
    slot_id = lax.broadcasted_iota(jnp.int32, (n_heads, span), 1)
    same_group = (head_id // group) == (slot_id // ctx)
    position = jnp.where(same_group, slot_id % ctx, ctx)

    def attend_rows(first):
        q_f = q_rows[first : first + BATCH].reshape(tall, hd)
        q_b = q_f.astype(bf16)
        each = range(BATCH)
        kv = [cache_v[first + i] for i in each]
        scores = jnp.concatenate(
            [
                lax.dot_general(
                    q_b[i * n_heads : (i + 1) * n_heads],
                    kv[i][:, :hd],
                    (((1,), (1,)), ((), ())),
                    preferred_element_type=f32,
                )
                for i in each
            ],
            0,
        )
        scores = scores * scale
        fresh_kv = jnp.concatenate(
            [
                jnp.broadcast_to(
                    new_ref[first + i].astype(f32)[:, None, :], (kvh, group, 2 * hd)
                ).reshape(n_heads, 2 * hd)
                for i in each
            ],
            0,
        )
        fresh = jnp.sum(q_f * fresh_kv[:, :hd], 1, keepdims=True) * scale
        valid = jnp.concatenate(
            [jnp.where(position < len_ref[first + i], 1.0, 0.0) for i in each], 0
        ) > 0.5
        masked = jnp.where(valid, scores, -1e30)
        top = jnp.maximum(jnp.max(masked, 1, keepdims=True), fresh)
        terms = jnp.where(valid, jnp.exp(masked - top), 0.0)
        fresh_term = jnp.exp(fresh - top)
        total = jnp.sum(terms, 1, keepdims=True) + fresh_term
        weights = (terms / total).astype(bf16)
        fresh_weight = (fresh_term / total).astype(bf16).astype(f32)
        mixed = jnp.concatenate(
            [
                jnp.dot(
                    weights[i * n_heads : (i + 1) * n_heads],
                    kv[i][:, hd:],
                    preferred_element_type=f32,
                )
                for i in each
            ],
            0,
        )
        mixed = mixed + fresh_weight * fresh_kv[:, hd:]
        o_rows[first : first + BATCH] = mixed.reshape(BATCH, n_heads, hd)

    part = rows_att // 2

    def place_heads(owner, first, dst, at):
        for i in range(0, half_heads, 8):
            start = pl.multiple_of(owner * half_heads + i, 8)
            by_head = jnp.transpose(o_rows[first : first + part, pl.ds(start, 8), :], (1, 0, 2))
            by_head = by_head.astype(bf16)
            for j in range(8):
                dst[at, (i + j) * hd : (i + j + 1) * hd] = by_head[j]

    head_copies = []
    for p in range(2):
        for first in range(p * part, (p + 1) * part, BATCH):
            attend_rows(first)
        if p == 0:
            pl.semaphore_wait(barrier, ep_size)
        here = pl.ds(p * part, part)
        there = pl.ds(pl.multiple_of(tp * rows_att + p * part, part), part)
        place_heads(other_tp, p * part, heads_out, here)
        copy = push(
            heads_out.at[here, :], heads.at[there, :], head_s.at[p], head_r.at[p], {"tp": other_tp}
        )
        copy.start()
        head_copies.append(copy)
        place_heads(tp, p * part, heads, there)

    route_copies = []
    for step in range(1, ep_size):
        copy = push(
            route.at[ep],
            route.at[ep],
            route_s.at[step],
            route_r.at[step],
            {"ep": lax.rem(ep + step, ep_size)},
        )
        copy.start()
        route_copies.append(copy)

    loads[1].wait()
    for copy in head_copies:
        copy.wait()

    chunks = part_out.shape[0]
    chunk = half // chunks
    part_copies = []
    for i in range(chunks):
        def project(j, carry, i=i):
            at = pl.multiple_of(j * TILE, TILE)
            cols = pl.ds(pl.multiple_of(other_tp * half + i * chunk + at, TILE), TILE)
            part_out[i, :, pl.ds(at, TILE)] = jnp.dot(
                heads[...], out_w[:, cols], preferred_element_type=f32
            ).astype(bf16)
            return carry

        lax.fori_loop(0, chunk // TILE, project, 0)
        copy = push(
            part_out.at[i], part_in.at[i], part_s.at[i], part_r.at[i], {"tp": other_tp}
        )
        copy.start()
        part_copies.append(copy)

    def project_own(j, carry):
        at = pl.multiple_of(j * TILE, TILE)
        cols = pl.ds(pl.multiple_of(tp * half + at, TILE), TILE)
        own_part[:, pl.ds(at, TILE)] = jnp.dot(
            heads[...], out_w[:, cols], preferred_element_type=f32
        ) + resid_ref[:, pl.ds(at, TILE)].astype(f32)
        return carry

    lax.fori_loop(0, half // TILE, project_own, 0)

    squares = jnp.zeros((rows, 1), f32)
    for i in range(chunks):
        part_copies[i].wait()
        cols = slice(i * chunk, (i + 1) * chunk)
        total = (own_part[:, cols] + part_in[i].astype(f32)).astype(bf16)
        hidden[:, cols] = total
        total = total.astype(f32)
        squares = squares + jnp.sum(total * total, 1, keepdims=True)
    wide = jnp.broadcast_to(squares, (rows, 128))
    if rows < 128:
        wide = jnp.concatenate([wide, jnp.zeros((128 - rows, 128), f32)], 0)
    sq_out[...] = jnp.transpose(wide)[:8]
    sq_copy = push(sq_out, sq_in, sq_s, sq_r, {"tp": other_tp})
    sq_copy.start()
    my_cols = pl.ds(pl.multiple_of(tp * half, half), half)
    their_cols = pl.ds(pl.multiple_of(other_tp * half, half), half)
    gain = gain_ref[:, my_cols]

    def block(chip, which, cols):
        return normed.at[pl.ds(pl.multiple_of((chip * CORES + which) * rows, rows), rows), cols]

    own_block = block(line, core, my_cols)
    own_block[...] = (hidden[...].astype(f32) * gain).astype(bf16)

    lines = [None]
    for step in range(1, chips):
        copy = push(
            own_block,
            own_block,
            line_s.at[step],
            line_r.at[step],
            {"ep": lax.rem(line + step, chips) * CORES + core},
        )
        copy.start()
        lines.append(copy)
    sources = [lax.rem(line + chips - step, chips) for step in range(chips)]
    cores, sides, forwards = {}, {}, {}

    def spread(k):
        if k > 0:
            lines[k].wait_recv()
        here = block(sources[k], core, my_cols)
        sides[k] = push(here, here, side_s.at[k], side_r.at[k], {"tp": other_tp})
        sides[k].start()
        cores[k] = push(here, here, core_s.at[k], core_r.at[k], {"ep": other_core})
        cores[k].start()

    def forward(k):
        sides[k].wait_recv()
        there = block(sources[k], core, their_cols)
        forwards[k] = push(there, there, fwd_s.at[k], fwd_r.at[k], {"ep": other_core})
        forwards[k].start()

    pairs, backs, rets = {}, {}, {}
    expert = CORES * ep + tp

    def column(table, owner, at):
        row = table[owner, pl.ds(at, 1), :]
        return jnp.transpose(jnp.broadcast_to(row, (128, 128)))[:rows, :1]

    low = pl.ds(pl.multiple_of((1 - core) * rows, rows), rows)
    high = pl.ds(pl.multiple_of(core * rows, rows), rows)

    def feed(k):
        cores[k].wait_recv()
        forwards[k].wait_recv()
        first = pl.multiple_of(sources[k] * (CORES * rows), CORES * rows)
        both = pl.ds(first, CORES * rows)
        scaling = jnp.concatenate(
            [column(inv_rows, sources[k] * CORES + i, 0) for i in range(CORES)], 0
        )

        def up_tile(j, carry):
            cols = pl.ds(pl.multiple_of(j * TILE, TILE), TILE)
            values = normed[both, :]
            gate_proj = jnp.dot(values, w_gate[:, cols], preferred_element_type=f32) * scaling
            up_proj = jnp.dot(values, w_up[:, cols], preferred_element_type=f32) * scaling
            silu = gate_proj / (1.0 + jnp.exp(-gate_proj))
            both_rows = (silu * up_proj).astype(bf16)
            activated[low, cols] = both_rows[:rows]
            activated[high, cols] = both_rows[rows:]
            return carry

        lax.fori_loop(0, hidden_units // TILE, up_tile, 0)
        keep_weight = column(route, sources[k] * CORES + core, expert)
        give_weight = column(route, sources[k] * CORES + 1 - core, expert)

        for h, owner in enumerate((other_tp, tp)):
            def down_tile(j, carry, h=h, owner=owner):
                at = pl.multiple_of(j * TILE, TILE)
                cols = pl.ds(pl.multiple_of(owner * half + at, TILE), TILE)
                value = jnp.dot(activated[...], w_down[:, cols], preferred_element_type=f32)
                pair_out[k, h, :, pl.ds(at, TILE)] = (value[:rows] * give_weight).astype(bf16)
                pair_keep[k, h, :, pl.ds(at, TILE)] = value[rows:] * keep_weight
                return carry

            lax.fori_loop(0, half // TILE, down_tile, 0)
            pairs[k, h] = push(
                pair_out.at[k, h],
                pair_in.at[k, h],
                pair_s.at[k, h],
                pair_r.at[k, h],
                {"ep": other_core},
            )
            pairs[k, h].start()

    def cross(k):
        pairs[k, 0].wait_recv()
        side_out[k] = (pair_keep[k, 0] + pair_in[k, 0].astype(f32)).astype(bf16)
        backs[k] = push(
            side_out.at[k], side_in.at[k], back_s.at[k], back_r.at[k], {"tp": other_tp}
        )
        backs[k].start()

    def keep(k):
        pairs[k, 1].wait_recv()
        side_keep[k] = pair_keep[k, 1] + pair_in[k, 1].astype(f32)

    def give_back(k):
        backs[k].wait_recv()
        total = side_keep[k] + side_in[k].astype(f32)
        if k == 0:
            side_keep[k] = total + hidden[...].astype(f32)
            return
        line_out[k] = total.astype(bf16)
        rets[k] = push(
            line_out.at[k],
            line_in.at[k],
            ret_s.at[k],
            ret_r.at[k],
            {"ep": sources[k] * CORES + core},
        )
        rets[k].start()

    spread(0)
    sq_copy.wait()
    inv_rows[ep] = lax.rsqrt((sq_out[...] + sq_in[...]) / width + epsilon)
    for step in range(1, ep_size):
        copy = push(
            inv_rows.at[ep],
            inv_rows.at[ep],
            inv_s.at[step],
            inv_r.at[step],
            {"ep": lax.rem(ep + step, ep_size)},
        )
        copy.start()
        route_copies.append(copy)
    forward(0)
    for copy in route_copies:
        copy.wait()
    for load in loads[2:]:
        load.wait()
    for k in range(chips):
        if k + 1 < chips:
            spread(k + 1)
        feed(k)
        if k + 1 < chips:
            forward(k + 1)
        if k > 0:
            keep(k - 1)
            give_back(k - 1)
        cross(k)
    keep(chips - 1)
    give_back(chips - 1)
    result = side_keep[0]
    for k in range(1, chips):
        rets[k].wait_recv()
        result = result + line_in[k].astype(f32)
    out_ref[...] = result.astype(bf16)
    for k in range(chips):
        cores[k].wait_send()
        sides[k].wait_send()
        forwards[k].wait_send()
        pairs[k, 0].wait_send()
        pairs[k, 1].wait_send()
        backs[k].wait_send()
        if k > 0:
            lines[k].wait_send()
            rets[k].wait_send()


def fused(
    queries,
    new_kv,
    cache,
    lengths,
    out_weight,
    residual,
    norm_gain,
    expert_ids,
    expert_gates,
    w_gate,
    w_up,
    w_down,
):
    f32, bf16 = jnp.float32, jnp.bfloat16
    ep_size = lax.axis_size("ep")
    chips = ep_size // CORES
    rows_att, in_width = queries.shape
    kvh, ctx, kv_width = cache.shape[1:]
    hd = kv_width // 2
    group = in_width // (hd * kvh)
    rows, half = residual.shape
    width = 2 * half
    experts = ep_size * EXP_DEV
    chunks = 2
    vmem = pl.BlockSpec(memory_space=pltpu.VMEM)
    hbm = pl.BlockSpec(memory_space=pl.ANY)
    smem = pl.BlockSpec(memory_space=pltpu.SMEM)
    V = pltpu.VMEM
    dma = pltpu.SemaphoreType.DMA
    scratch = [
        V((rows_att, kvh * ctx, kv_width), bf16),
        V(out_weight.shape, bf16),
        V(w_gate.shape, bf16),
        V(w_up.shape, bf16),
        V(w_down.shape, bf16),
        V((rows_att, in_width // hd, hd), f32),
        V((rows_att, in_width // hd, hd), f32),
        V((rows_att, in_width // 2), bf16),
        V((rows, in_width // 2), bf16),
        V((chunks, rows, half // chunks), bf16),
        V((chunks, rows, half // chunks), bf16),
        V((rows, half), f32),
        V((rows, half), bf16),
        V((8, 128), f32),
        V((8, 128), f32),
        V((ep_size, 8, 128), f32),
        V((ep_size, experts, 128), f32),
        V((ep_size * rows, width), bf16),
        V((CORES * rows, w_down.shape[0]), bf16),
        V((chips, 2, rows, half), f32),
        V((chips, 2, rows, half), bf16),
        V((chips, 2, rows, half), bf16),
        V((chips, rows, half), f32),
        V((chips, rows, half), bf16),
        V((chips, rows, half), bf16),
        V((chips, rows, half), bf16),
        V((chips, rows, half), bf16),
        dma((5,)),
        dma((ep_size,)),
        dma((ep_size,)),
        dma((2,)),
        dma((2,)),
        dma((chunks,)),
        dma((chunks,)),
        dma,
        dma,
        dma((ep_size,)),
        dma((ep_size,)),
    ] + [dma((chips,)) for _ in range(8)] + [dma((chips, 2))] * 2 + [dma((chips,)) for _ in range(4)]
    return pl.pallas_call(
        functools.partial(layer_kernel, ep_size, kvh),
        out_shape=jax.ShapeDtypeStruct((rows, half), bf16),
        in_specs=[vmem, vmem, smem, vmem, vmem, vmem, vmem, hbm, hbm, hbm, hbm, hbm],
        out_specs=vmem,
        scratch_shapes=scratch,
        compiler_params=pltpu.CompilerParams(
            collective_id=0, has_side_effects=True, vmem_limit_bytes=56 * 1024 * 1024
        ),
    )(
        queries,
        new_kv,
        lengths,
        residual,
        norm_gain.reshape(1, width),
        expert_ids.T,
        expert_gates.T,
        cache.reshape(rows_att, kvh * ctx, kv_width),
        out_weight,
        w_gate,
        w_up,
        w_down,
    )


def solution(mesh):
    in_specs = (
        P(("groups", "ep", "tp"), None),
        P(("groups", "ep", "tp"), None, None),
        P(("groups", "ep", "tp"), None, None, None),
        P(("groups", "ep", "tp")),
        P("tp", None),
        P(("groups", "ep"), "tp"),
        P(),
        P(("groups", "ep"), None),
        P(("groups", "ep"), None),
        P(None, ("ep", "tp")),
        P(None, ("ep", "tp")),
        P(("ep", "tp"), None),
    )
    out_specs = P(("groups", "ep"), "tp")
    body = fused if mesh.shape["tp"] == EXP_DEV else per_device
    return jax.shard_map(
        body, mesh=mesh, in_specs=in_specs, out_specs=out_specs, check_vma=False
    )
```

```python
import functools
import math

import jax
import jax.numpy as jnp
from jax import lax
from jax.experimental import pallas as pl
from jax.experimental.pallas import tpu as pltpu
from jax.sharding import PartitionSpec as P

MESH = pl.DeviceIdType.MESH
CORES = 2
TILE = 256
BATCH = 4

D = 2048
TOPK = 8
EXP_DEV = 2


epsilon = 1e-06


def attend(queries, new_kv, cache, lengths):
    row_count = queries.shape[0]
    kv_local = cache.shape[1]
    positions = cache.shape[2]
    head_dim = cache.shape[3] // 2
    group_size = queries.shape[1] // (head_dim * kv_local)
    query = queries.reshape(row_count, kv_local, group_size, head_dim)
    key_part = cache[..., :head_dim]
    value_part = cache[..., head_dim:]
    score_scale = 1.0 / math.sqrt(head_dim)
    scores = (
        jnp.einsum("rgqd,rgcd->rgqc", query, key_part, preferred_element_type=jnp.float32)
        * score_scale
    )
    fresh_score = (
        jnp.einsum(
            "rgqd,rgd->rgq", query, new_kv[..., :head_dim], preferred_element_type=jnp.float32
        )
        * score_scale
    )
    is_valid = (jnp.arange(positions, dtype=jnp.int32)[None, :] < lengths[:, None])[
        :, None, None, :
    ]
    masked = jnp.where(is_valid, scores, -1e30)
    row_max = jnp.maximum(jnp.max(masked, -1), fresh_score)
    exp_terms = jnp.where(is_valid, jnp.exp(masked - row_max[..., None]), 0.0)
    fresh_exp = jnp.exp(fresh_score - row_max)
    totals = jnp.sum(exp_terms, -1) + fresh_exp
    weights = (exp_terms / totals[..., None]).astype(jnp.bfloat16)
    fresh_weight = (fresh_exp / totals).astype(jnp.bfloat16)
    mixed = jnp.einsum("rgqc,rgcd->rgqd", weights, value_part, preferred_element_type=jnp.float32)
    mixed = mixed + fresh_weight.astype(jnp.float32)[..., None] * new_kv[
        :, :, None, head_dim:
    ].astype(jnp.float32)
    return mixed.astype(jnp.bfloat16).reshape(row_count, kv_local * group_size * head_dim)


def slot_tables(expert_ids, expert_gates, experts, capacity):
    route_weights = expert_gates / jnp.sum(expert_gates, 1, keepdims=True)
    matches = expert_ids[:, :, None] == jnp.arange(experts, dtype=jnp.int32)[None, None, :]
    chosen = jnp.any(matches, 1)
    slot_rank = jnp.cumsum(chosen.astype(jnp.int32), 0) - 1
    slot_map = chosen[None] & (
        slot_rank[None] == jnp.arange(capacity, dtype=jnp.int32)[:, None, None]
    )
    return (slot_map, slot_rank, route_weights)


def run_expert(gathered, w_gate, w_up, w_down):
    gate_proj = jnp.einsum("qcd,df->qcf", gathered, w_gate, preferred_element_type=jnp.float32)
    up_proj = jnp.einsum("qcd,df->qcf", gathered, w_up, preferred_element_type=jnp.float32)
    activated = (jax.nn.silu(gate_proj) * up_proj).astype(jnp.bfloat16)
    projected = jnp.einsum("qcf,fd->qcd", activated, w_down, preferred_element_type=jnp.float32)
    return lax.all_to_all(
        projected.astype(jnp.bfloat16), "ep", split_axis=0, concat_axis=0, tiled=True
    ).astype(projected.dtype)


def per_device(
    queries,
    new_kv,
    cache,
    lengths,
    out_weight,
    residual,
    norm_gain,
    expert_ids,
    expert_gates,
    w_gate,
    w_up,
    w_down,
):
    row_count = residual.shape[0]
    col_width = residual.shape[1]
    ep_size = lax.axis_size("ep")
    tp_size = lax.axis_size("tp")
    tp_rank = lax.axis_index("tp")
    experts = ep_size * EXP_DEV
    capacity = min(row_count, 2 * row_count * TOPK // experts)
    pieces = tp_size // EXP_DEV
    parity = tp_rank // pieces
    attn_local = attend(queries, new_kv, cache, lengths)
    attn_heads = lax.all_to_all(attn_local, "tp", split_axis=1, concat_axis=0, tiled=True)
    partial_value = jnp.dot(attn_heads, out_weight, preferred_element_type=jnp.float32)
    normed_full = None
    normed_share = None
    head_share = lax.psum_scatter(partial_value, "tp", scatter_dimension=1, tiled=True)
    hidden_share = (residual.astype(jnp.float32) + head_share).astype(jnp.bfloat16)
    hidden_f = hidden_share.astype(jnp.float32)
    squares = lax.psum(jnp.sum(hidden_f * hidden_f, 1, keepdims=True), "tp")
    inv_scale = lax.rsqrt(squares / D + epsilon)
    gain_share = lax.dynamic_slice_in_dim(norm_gain, tp_rank * col_width, col_width)
    normed_share = (hidden_f * inv_scale * gain_share).astype(jnp.bfloat16)
    slot_map, slot_rank, route_weights = slot_tables(expert_ids, expert_gates, experts, capacity)
    slot_grid = slot_map.reshape(capacity, row_count, ep_size, EXP_DEV)
    own_slots = lax.dynamic_index_in_dim(slot_grid, parity, 3, keepdims=False)
    normed_full = lax.all_gather(normed_share, "tp", axis=1, tiled=True)
    outgoing = jnp.einsum(
        "crq,rd->qcd",
        own_slots.astype(jnp.bfloat16),
        normed_full,
        preferred_element_type=jnp.float32,
    ).astype(jnp.bfloat16)
    returned = run_expert(
        lax.all_to_all(outgoing, "ep", split_axis=0, concat_axis=0, tiled=True),
        w_gate,
        w_up,
        w_down,
    )
    picked_rank = jnp.take_along_axis(slot_rank, expert_ids, 1)
    owner = expert_ids // EXP_DEV
    member = expert_ids % EXP_DEV
    flat = returned.reshape(ep_size * capacity, returned.shape[-1])
    index = owner * capacity + picked_rank
    weight = jnp.where(member == parity, route_weights, 0.0)
    moe_part = jnp.sum(weight[:, :, None] * flat[index], 1)
    moe_share = lax.psum_scatter(
        moe_part.astype(jnp.bfloat16), "tp", scatter_dimension=1, tiled=True
    ).astype(jnp.float32)
    return (hidden_share.astype(jnp.float32) + moe_share).astype(jnp.bfloat16)


def layer_kernel(
    ep_size,
    kvh,
    q_ref,
    new_ref,
    len_ref,
    resid_ref,
    gain_ref,
    ids_ref,
    gates_ref,
    cache_hbm,
    out_w_hbm,
    gate_hbm,
    up_hbm,
    down_hbm,
    out_ref,
    cache_v,
    out_w,
    w_gate,
    w_up,
    w_down,
    q_rows,
    o_rows,
    heads_out,
    heads,
    part_out,
    part_in,
    own_part,
    hidden,
    sq_out,
    sq_in,
    route,
    normed,
    activated,
    pair_keep,
    pair_out,
    pair_in,
    side_keep,
    side_out,
    side_in,
    line_out,
    line_in,
    load_sem,
    route_s,
    route_r,
    head_s,
    head_r,
    part_s,
    part_r,
    sq_s,
    sq_r,
    line_s,
    line_r,
    core_s,
    core_r,
    side_s,
    side_r,
    fwd_s,
    fwd_r,
    pair_s,
    pair_r,
    back_s,
    back_r,
    ret_s,
    ret_r,
):
    f32, bf16 = jnp.float32, jnp.bfloat16
    ep = lax.axis_index("ep")
    tp = lax.axis_index("tp")
    core = lax.rem(ep, CORES)
    line = lax.div(ep, CORES)
    chips = ep_size // CORES
    other_core = ep + 1 - 2 * core
    other_tp = 1 - tp
    rows_att = q_ref.shape[0]
    rows = resid_ref.shape[0]
    half = resid_ref.shape[1]
    width = 2 * half
    hd = new_ref.shape[2] // 2
    n_heads = q_ref.shape[1] // hd
    group = n_heads // kvh
    ctx = cache_v.shape[1] // kvh
    experts = route.shape[1]
    half_heads = n_heads // 2
    half_in = half_heads * hd
    hidden_units = w_down.shape[0]

    loads = [
        pltpu.make_async_copy(src, dst, load_sem.at[i])
        for i, (src, dst) in enumerate(
            (
                (cache_hbm, cache_v),
                (out_w_hbm, out_w),
                (gate_hbm, w_gate),
                (up_hbm, w_up),
                (down_hbm, w_down),
            )
        )
    ]
    for load in loads:
        load.start()

    barrier = pltpu.get_barrier_semaphore()
    for step in range(1, ep_size):
        pl.semaphore_signal(
            barrier,
            inc=1,
            device_id={"ep": lax.rem(ep + step, ep_size)},
            device_id_type=MESH,
        )
    pl.semaphore_signal(barrier, inc=1, device_id={"tp": other_tp}, device_id_type=MESH)

    def push(src, dst, send, recv, target):
        return pltpu.make_async_remote_copy(
            src_ref=src,
            dst_ref=dst,
            send_sem=send,
            recv_sem=recv,
            device_id=target,
            device_id_type=MESH,
        )

    sent = []

    gates = gates_ref[...]
    shares = gates / jnp.sum(gates, 0, keepdims=True)
    ids = ids_ref[...]
    expert_id = lax.broadcasted_iota(jnp.int32, (experts, rows), 0)
    dense = jnp.zeros((experts, rows), f32)
    for k in range(TOPK):
        dense = dense + jnp.where(ids[k : k + 1] == expert_id, shares[k : k + 1], 0.0)
    if rows < 128:
        dense = jnp.concatenate([dense, jnp.zeros((experts, 128 - rows), f32)], 1)
    route[ep] = dense

    for h in range(0, n_heads, 8):
        by_head = jnp.stack([q_ref[:, i * hd : (i + 1) * hd].astype(f32) for i in range(h, h + 8)])
        q_rows[:, h : h + 8, :] = jnp.transpose(by_head, (1, 0, 2))

    scale = 1.0 / math.sqrt(hd)
    loads[0].wait()
    span = kvh * ctx
    tall = BATCH * n_heads
    head_id = lax.broadcasted_iota(jnp.int32, (n_heads, span), 0)
    slot_id = lax.broadcasted_iota(jnp.int32, (n_heads, span), 1)
    same_group = (head_id // group) == (slot_id // ctx)
    position = jnp.where(same_group, slot_id % ctx, ctx)

    def attend_rows(first):
        q_f = q_rows[first : first + BATCH].reshape(tall, hd)
        q_b = q_f.astype(bf16)
        each = range(BATCH)
        kv = [cache_v[first + i] for i in each]
        scores = jnp.concatenate(
            [
                lax.dot_general(
                    q_b[i * n_heads : (i + 1) * n_heads],
                    kv[i][:, :hd],
                    (((1,), (1,)), ((), ())),
                    preferred_element_type=f32,
                )
                for i in each
            ],
            0,
        )
        scores = scores * scale
        fresh_kv = jnp.concatenate(
            [
                jnp.broadcast_to(
                    new_ref[first + i].astype(f32)[:, None, :], (kvh, group, 2 * hd)
                ).reshape(n_heads, 2 * hd)
                for i in each
            ],
            0,
        )
        fresh = jnp.sum(q_f * fresh_kv[:, :hd], 1, keepdims=True) * scale
        valid = jnp.concatenate(
            [jnp.where(position < len_ref[first + i], 1.0, 0.0) for i in each], 0
        ) > 0.5
        masked = jnp.where(valid, scores, -1e30)
        top = jnp.maximum(jnp.max(masked, 1, keepdims=True), fresh)
        terms = jnp.where(valid, jnp.exp(masked - top), 0.0)
        fresh_term = jnp.exp(fresh - top)
        total = jnp.sum(terms, 1, keepdims=True) + fresh_term
        weights = (terms / total).astype(bf16)
        fresh_weight = (fresh_term / total).astype(bf16).astype(f32)
        mixed = jnp.concatenate(
            [
                jnp.dot(
                    weights[i * n_heads : (i + 1) * n_heads],
                    kv[i][:, hd:],
                    preferred_element_type=f32,
                )
                for i in each
            ],
            0,
        )
        mixed = mixed + fresh_weight * fresh_kv[:, hd:]
        o_rows[first : first + BATCH] = mixed.reshape(BATCH, n_heads, hd)

    part = rows_att // 2

    def place_heads(owner, first, dst, at):
        for i in range(0, half_heads, 8):
            start = pl.multiple_of(owner * half_heads + i, 8)
            by_head = jnp.transpose(o_rows[first : first + part, pl.ds(start, 8), :], (1, 0, 2))
            by_head = by_head.astype(bf16)
            for j in range(8):
                dst[at, (i + j) * hd : (i + j + 1) * hd] = by_head[j]

    head_copies = []
    for p in range(2):
        for first in range(p * part, (p + 1) * part, BATCH):
            attend_rows(first)
        if p == 0:
            pl.semaphore_wait(barrier, ep_size)
        here = pl.ds(p * part, part)
        there = pl.ds(pl.multiple_of(tp * rows_att + p * part, part), part)
        place_heads(other_tp, p * part, heads_out, here)
        copy = push(
            heads_out.at[here, :], heads.at[there, :], head_s.at[p], head_r.at[p], {"tp": other_tp}
        )
        copy.start()
        head_copies.append(copy)
        place_heads(tp, p * part, heads, there)

    route_copies = []
    for step in range(1, ep_size):
        copy = push(
            route.at[ep],
            route.at[ep],
            route_s.at[step],
            route_r.at[step],
            {"ep": lax.rem(ep + step, ep_size)},
        )
        copy.start()
        route_copies.append(copy)

    loads[1].wait()
    for copy in head_copies:
        copy.wait()

    chunks = part_out.shape[0]
    chunk = half // chunks
    part_copies = []
    for i in range(chunks):
        def project(j, carry, i=i):
            at = pl.multiple_of(j * TILE, TILE)
            cols = pl.ds(pl.multiple_of(other_tp * half + i * chunk + at, TILE), TILE)
            part_out[i, :, pl.ds(at, TILE)] = jnp.dot(
                heads[...], out_w[:, cols], preferred_element_type=f32
            ).astype(bf16)
            return carry

        lax.fori_loop(0, chunk // TILE, project, 0)
        copy = push(
            part_out.at[i], part_in.at[i], part_s.at[i], part_r.at[i], {"tp": other_tp}
        )
        copy.start()
        part_copies.append(copy)

    def project_own(j, carry):
        at = pl.multiple_of(j * TILE, TILE)
        cols = pl.ds(pl.multiple_of(tp * half + at, TILE), TILE)
        own_part[:, pl.ds(at, TILE)] = jnp.dot(
            heads[...], out_w[:, cols], preferred_element_type=f32
        ) + resid_ref[:, pl.ds(at, TILE)].astype(f32)
        return carry

    lax.fori_loop(0, half // TILE, project_own, 0)

    squares = jnp.zeros((rows, 1), f32)
    for i in range(chunks):
        part_copies[i].wait()
        cols = slice(i * chunk, (i + 1) * chunk)
        total = (own_part[:, cols] + part_in[i].astype(f32)).astype(bf16)
        hidden[:, cols] = total
        total = total.astype(f32)
        squares = squares + jnp.sum(total * total, 1, keepdims=True)
    sq_out[...] = jnp.broadcast_to(squares, sq_out.shape)
    sq_copy = push(sq_out, sq_in, sq_s, sq_r, {"tp": other_tp})
    sq_copy.start()
    my_cols = pl.ds(pl.multiple_of(tp * half, half), half)
    their_cols = pl.ds(pl.multiple_of(other_tp * half, half), half)
    gain = gain_ref[:, my_cols]
    sq_copy.wait()
    inv = lax.rsqrt((squares + sq_in[:, :1]) / width + epsilon)

    def block(chip, which, cols):
        return normed.at[pl.ds(pl.multiple_of((chip * CORES + which) * rows, rows), rows), cols]

    own_block = block(line, core, my_cols)
    own_block[...] = (hidden[...].astype(f32) * inv * gain).astype(bf16)

    lines = [None]
    for step in range(1, chips):
        copy = push(
            own_block,
            own_block,
            line_s.at[step],
            line_r.at[step],
            {"ep": lax.rem(line + step, chips) * CORES + core},
        )
        copy.start()
        lines.append(copy)
    sources = [lax.rem(line + chips - step, chips) for step in range(chips)]
    cores, sides, forwards = {}, {}, {}

    def spread(k):
        if k > 0:
            lines[k].wait_recv()
        here = block(sources[k], core, my_cols)
        sides[k] = push(here, here, side_s.at[k], side_r.at[k], {"tp": other_tp})
        sides[k].start()
        cores[k] = push(here, here, core_s.at[k], core_r.at[k], {"ep": other_core})
        cores[k].start()

    def forward(k):
        sides[k].wait_recv()
        there = block(sources[k], core, their_cols)
        forwards[k] = push(there, there, fwd_s.at[k], fwd_r.at[k], {"ep": other_core})
        forwards[k].start()

    pairs, backs, rets = {}, {}, {}
    expert = CORES * ep + tp

    def column(owner):
        row = route[owner, pl.ds(expert, 1), :]
        return jnp.transpose(jnp.broadcast_to(row, (128, 128)))[:rows, :1]

    low = pl.ds(pl.multiple_of((1 - core) * rows, rows), rows)
    high = pl.ds(pl.multiple_of(core * rows, rows), rows)

    def feed(k):
        cores[k].wait_recv()
        forwards[k].wait_recv()
        first = pl.multiple_of(sources[k] * (CORES * rows), CORES * rows)
        both = pl.ds(first, CORES * rows)

        def up_tile(j, carry):
            cols = pl.ds(pl.multiple_of(j * TILE, TILE), TILE)
            values = normed[both, :]
            gate_proj = jnp.dot(values, w_gate[:, cols], preferred_element_type=f32)
            up_proj = jnp.dot(values, w_up[:, cols], preferred_element_type=f32)
            silu = gate_proj / (1.0 + jnp.exp(-gate_proj))
            both_rows = (silu * up_proj).astype(bf16)
            activated[low, cols] = both_rows[:rows]
            activated[high, cols] = both_rows[rows:]
            return carry

        lax.fori_loop(0, hidden_units // TILE, up_tile, 0)
        keep_weight = column(sources[k] * CORES + core)
        give_weight = column(sources[k] * CORES + 1 - core)

        for h, owner in enumerate((other_tp, tp)):
            def down_tile(j, carry, h=h, owner=owner):
                at = pl.multiple_of(j * TILE, TILE)
                cols = pl.ds(pl.multiple_of(owner * half + at, TILE), TILE)
                value = jnp.dot(activated[...], w_down[:, cols], preferred_element_type=f32)
                pair_out[k, h, :, pl.ds(at, TILE)] = (value[:rows] * give_weight).astype(bf16)
                pair_keep[k, h, :, pl.ds(at, TILE)] = value[rows:] * keep_weight
                return carry

            lax.fori_loop(0, half // TILE, down_tile, 0)
            pairs[k, h] = push(
                pair_out.at[k, h],
                pair_in.at[k, h],
                pair_s.at[k, h],
                pair_r.at[k, h],
                {"ep": other_core},
            )
            pairs[k, h].start()

    def cross(k):
        pairs[k, 0].wait_recv()
        side_out[k] = (pair_keep[k, 0] + pair_in[k, 0].astype(f32)).astype(bf16)
        backs[k] = push(
            side_out.at[k], side_in.at[k], back_s.at[k], back_r.at[k], {"tp": other_tp}
        )
        backs[k].start()

    def keep(k):
        pairs[k, 1].wait_recv()
        side_keep[k] = pair_keep[k, 1] + pair_in[k, 1].astype(f32)

    def give_back(k):
        backs[k].wait_recv()
        total = side_keep[k] + side_in[k].astype(f32)
        if k == 0:
            side_keep[k] = total + hidden[...].astype(f32)
            return
        line_out[k] = total.astype(bf16)
        rets[k] = push(
            line_out.at[k],
            line_in.at[k],
            ret_s.at[k],
            ret_r.at[k],
            {"ep": sources[k] * CORES + core},
        )
        rets[k].start()

    spread(0)
    for copy in route_copies:
        copy.wait()
    for load in loads[2:]:
        load.wait()
    forward(0)
    for k in range(chips):
        if k + 1 < chips:
            spread(k + 1)
        feed(k)
        if k + 1 < chips:
            forward(k + 1)
        if k > 0:
            keep(k - 1)
            give_back(k - 1)
        cross(k)
    keep(chips - 1)
    give_back(chips - 1)
    result = side_keep[0]
    for k in range(1, chips):
        rets[k].wait_recv()
        result = result + line_in[k].astype(f32)
    out_ref[...] = result.astype(bf16)
    for k in range(chips):
        cores[k].wait_send()
        sides[k].wait_send()
        forwards[k].wait_send()
        pairs[k, 0].wait_send()
        pairs[k, 1].wait_send()
        backs[k].wait_send()
        if k > 0:
            lines[k].wait_send()
            rets[k].wait_send()


def fused(
    queries,
    new_kv,
    cache,
    lengths,
    out_weight,
    residual,
    norm_gain,
    expert_ids,
    expert_gates,
    w_gate,
    w_up,
    w_down,
):
    f32, bf16 = jnp.float32, jnp.bfloat16
    ep_size = lax.axis_size("ep")
    chips = ep_size // CORES
    rows_att, in_width = queries.shape
    kvh, ctx, kv_width = cache.shape[1:]
    hd = kv_width // 2
    group = in_width // (hd * kvh)
    rows, half = residual.shape
    width = 2 * half
    experts = ep_size * EXP_DEV
    chunks = 2
    vmem = pl.BlockSpec(memory_space=pltpu.VMEM)
    hbm = pl.BlockSpec(memory_space=pl.ANY)
    smem = pl.BlockSpec(memory_space=pltpu.SMEM)
    V = pltpu.VMEM
    dma = pltpu.SemaphoreType.DMA
    scratch = [
        V((rows_att, kvh * ctx, kv_width), bf16),
        V(out_weight.shape, bf16),
        V(w_gate.shape, bf16),
        V(w_up.shape, bf16),
        V(w_down.shape, bf16),
        V((rows_att, in_width // hd, hd), f32),
        V((rows_att, in_width // hd, hd), f32),
        V((rows_att, in_width // 2), bf16),
        V((rows, in_width // 2), bf16),
        V((chunks, rows, half // chunks), bf16),
        V((chunks, rows, half // chunks), bf16),
        V((rows, half), f32),
        V((rows, half), bf16),
        V((rows, 128), f32),
        V((rows, 128), f32),
        V((ep_size, experts, 128), f32),
        V((ep_size * rows, width), bf16),
        V((CORES * rows, w_down.shape[0]), bf16),
        V((chips, 2, rows, half), f32),
        V((chips, 2, rows, half), bf16),
        V((chips, 2, rows, half), bf16),
        V((chips, rows, half), f32),
        V((chips, rows, half), bf16),
        V((chips, rows, half), bf16),
        V((chips, rows, half), bf16),
        V((chips, rows, half), bf16),
        dma((5,)),
        dma((ep_size,)),
        dma((ep_size,)),
        dma((2,)),
        dma((2,)),
        dma((chunks,)),
        dma((chunks,)),
        dma,
        dma,
    ] + [dma((chips,)) for _ in range(8)] + [dma((chips, 2))] * 2 + [dma((chips,)) for _ in range(4)]
    return pl.pallas_call(
        functools.partial(layer_kernel, ep_size, kvh),
        out_shape=jax.ShapeDtypeStruct((rows, half), bf16),
        in_specs=[vmem, vmem, smem, vmem, vmem, vmem, vmem, hbm, hbm, hbm, hbm, hbm],
        out_specs=vmem,
        scratch_shapes=scratch,
        compiler_params=pltpu.CompilerParams(
            collective_id=0, has_side_effects=True, vmem_limit_bytes=56 * 1024 * 1024
        ),
    )(
        queries,
        new_kv,
        lengths,
        residual,
        norm_gain.reshape(1, width),
        expert_ids.T,
        expert_gates.T,
        cache.reshape(rows_att, kvh * ctx, kv_width),
        out_weight,
        w_gate,
        w_up,
        w_down,
    )


def solution(mesh):
    in_specs = (
        P(("groups", "ep", "tp"), None),
        P(("groups", "ep", "tp"), None, None),
        P(("groups", "ep", "tp"), None, None, None),
        P(("groups", "ep", "tp")),
        P("tp", None),
        P(("groups", "ep"), "tp"),
        P(),
        P(("groups", "ep"), None),
        P(("groups", "ep"), None),
        P(None, ("ep", "tp")),
        P(None, ("ep", "tp")),
        P(("ep", "tp"), None),
    )
    out_specs = P(("groups", "ep"), "tp")
    body = fused if mesh.shape["tp"] == EXP_DEV else per_device
    return jax.shard_map(
        body, mesh=mesh, in_specs=in_specs, out_specs=out_specs, check_vma=False
    )
```
